256 devices in a mesh: row: 32 (over y, z), col: 8 (over x, core).
Axes of the slice: x: 4, y: 4, z: 8, core: 2. Of those that a mesh axis runs over, the one named last changes fastest.
Arguments:
- tokens: bfloat16 [1024, 6144], P('col', 'row'), may hold values from -12 to 12
- out_grad: bfloat16 [1024, 6144], P('col', 'row'), may hold values from -12 to 12
- image_ids: int32 [1024], replicated, may hold values from 0 to 7, as said below
- learn_rate: float32 [1], replicated, may hold values from 2 to 16
- in_weight: float32 [6144, 24576], P('row', 'col'), may hold values from -6 to 6
- out_weight: float32 [24576, 6144], P('col', 'row'), may hold values from -6 to 6
Outputs:
- input_grad: bfloat16 [1024, 6144], P('col', 'row')
- in_weight_next: float32 [6144, 24576], P('row', 'col')
- out_weight_next: float32 [24576, 6144], P('col', 'row')
- example_norm: float32 [8], replicated
The draws below stay inside these ranges and needn't reach their ends.
Inputs may be any that keep to these rules, and one draw needn't show every extreme that they name: `image_ids`: each of the 8 images is named by exactly 128 tokens, in any order.
All inputs are finite; a program needn't handle non-finite values.
Results may differ from the reference program's by a relative error of at most 0.03.
Values may be sent and summed in bfloat16 or wider, within the bound.
No kernel may reach another device: no remote copies, remote signals or barrier semaphores. Data moves between devices by JAX's collectives and lax.ppermute only.
A program may use at most 128 MiB of HBM per device.

```python
import math
import jax
import jax.numpy as jnp
from jax import lax

D = 6144
FF = 24576
TOK_IMG = 128
TOKENS = 1024
IMAGES = 8
N_ROW = 32


def scaled_field(key, row_base, col_base, own_weight, shared_weight):
    own_key, shared_key = jax.random.split(key)
    windows = TOKENS // (2 * TOK_IMG)
    row_pos = jnp.arange(TOKENS, dtype=jnp.float32) / TOKENS - 0.5
    col_pos = jnp.arange(D, dtype=jnp.float32) / D - 0.5
    scales = (row_base ** row_pos)[:, None] * (col_base ** col_pos)[None, :]
    values = jnp.clip(jax.random.normal(own_key, (TOKENS, D), jnp.float32), -3.3, 3.3)
    shared = jnp.clip(jax.random.normal(shared_key, (windows, D), jnp.float32), -3.3, 3.3)
    spread_rows = jnp.repeat(shared, 2 * TOK_IMG, axis=0)
    return (own_weight * values + shared_weight * spread_rows) * scales


def draw_tokens(key, part):
    key = jax.random.fold_in(key, 11)
    return scaled_field(key, 3.0, 3.0, 0.85, 0.35).astype(jnp.bfloat16)


def draw_out_grad(key, part):
    key = jax.random.fold_in(key, 13)
    return scaled_field(key, 3.0, 3.0, 0.85, 0.35).astype(jnp.bfloat16)


def draw_image_ids(key, part):
    key = jax.random.fold_in(key, 7)
    block_key, window_key = jax.random.split(key)
    block_order = jax.random.permutation(block_key, TOKENS // TOK_IMG).astype(jnp.int32)
    base = block_order[jnp.arange(TOKENS, dtype=jnp.int32) // TOK_IMG]
    windows = TOKENS // (2 * TOK_IMG)
    keys = jax.random.split(window_key, windows)
    within = jax.vmap(lambda one_key: jax.random.permutation(one_key, 2 * TOK_IMG))(keys).astype(jnp.int32)
    offsets = (jnp.arange(windows, dtype=jnp.int32) * (2 * TOK_IMG))[:, None]
    positions = (within + offsets).reshape(TOKENS)
    return base[positions].astype(jnp.int32)


def levels(key, extent, shards, smallest, top_value):
    loudness = 1.0
    for position, shards_of in shards:
        heights = jax.random.uniform(jax.random.fold_in(jax.random.fold_in(key, 6), position), (shards_of,), jnp.float32, smallest / len(shards), top_value / len(shards))
        loudness = loudness * jnp.repeat(jnp.exp(heights), extent[position] // shards_of).reshape((-1,) + (1,) * (len(extent) - 1 - position))
    return loudness


def gaussian(rng, extent, scale, reach, cuts=(), kind=jnp.bfloat16):
    level = levels(rng, extent, cuts, -0.22, 0.18) if cuts else 1.0
    array = jax.random.normal(rng, extent, jnp.float32) * scale * level
    return jnp.minimum(jnp.maximum(array, -reach), reach).astype(kind)


def setup_inputs(seed: int = 0) -> dict:
    key_list = jax.random.split(jax.random.key(seed), 7)
    tokens = draw_tokens(jax.random.fold_in(key_list[6], 71), 0)
    out_grad = draw_out_grad(jax.random.fold_in(key_list[6], 71), 0)
    image_ids = draw_image_ids(jax.random.fold_in(key_list[6], 71), 0)
    learn_rate = jnp.clip(jnp.exp(jax.random.uniform(key_list[3], (1,), jnp.float32, math.log(2.0), math.log(16.0))), 2.0, 16.0)
    in_weight = gaussian(key_list[4], (D, FF), 1.0, 6.0, ((0, 32), (1, 8)), jnp.float32)
    out_weight = gaussian(key_list[5], (FF, D), 1.0, 6.0, ((0, 8), (1, 32)), jnp.float32)
    return dict(tokens=tokens, out_grad=out_grad, image_ids=image_ids, learn_rate=learn_rate, in_weight=in_weight, out_weight=out_weight)


root_half = 0.7071067811865476
inv_root_tau = 0.3989422804014327


def gelu_exact(value):
    return 0.5 * value * (1.0 + lax.erf(value * root_half))


def gelu_slope(value):
    return 0.5 * (1.0 + lax.erf(value * root_half)) + value * jnp.exp(-0.5 * value * value) * inv_root_tau


def rounded_partials(left_blocks, right_blocks, scale):
    def add_block(total, pieces):
        part = jnp.dot(pieces[0], pieces[1], preferred_element_type=jnp.float32) * scale
        half = lax.optimization_barrier(part.astype(jnp.bfloat16))
        return total + half.astype(jnp.float32), None

    start = jnp.zeros((left_blocks.shape[1], right_blocks.shape[2]), jnp.float32)
    total, _ = lax.scan(add_block, start, (left_blocks, right_blocks))
    return total


def gram(value):
    wide = value.astype(jnp.float32)
    return jnp.einsum("bti,bsi->bts", wide, wide)


def reference(tokens, out_grad, image_ids, learn_rate, in_weight, out_weight):
    scale_in = D ** -0.5
    scale_out = FF ** -0.5
    width_part = D // N_ROW
    in_half = in_weight.astype(jnp.bfloat16)
    out_half = out_weight.astype(jnp.bfloat16)
    tok_blocks = tokens.reshape(TOKENS, N_ROW, width_part).transpose(1, 0, 2)
    grad_blocks = out_grad.reshape(TOKENS, N_ROW, width_part).transpose(1, 0, 2)
    pre_act = rounded_partials(tok_blocks, in_half.reshape(N_ROW, width_part, FF), scale_in)
    act_half = gelu_exact(pre_act).astype(jnp.bfloat16)
    act_grad = rounded_partials(grad_blocks, out_half.reshape(FF, N_ROW, width_part).transpose(1, 2, 0), scale_out)
    hid_grad = (act_grad * gelu_slope(pre_act)).astype(jnp.bfloat16)
    input_grad = (jnp.dot(hid_grad, in_half.T, preferred_element_type=jnp.float32) * scale_in).astype(jnp.bfloat16)
    grad_in = jnp.dot(tokens.T, hid_grad, preferred_element_type=jnp.float32) * scale_in
    grad_out = jnp.dot(act_half.T, out_grad, preferred_element_type=jnp.float32) * scale_out
    order = jnp.argsort(image_ids, stable=True).astype(jnp.int32)

    def by_image(rows):
        return jnp.take(rows, order, axis=0).reshape(IMAGES, TOK_IMG, rows.shape[1])

    pair_in = gram(by_image(tokens)) * gram(by_image(hid_grad)) * (scale_in * scale_in)
    pair_out = gram(by_image(act_half)) * gram(by_image(out_grad)) * (scale_out * scale_out)
    example_sq = jnp.sum(pair_in + pair_out, axis=(1, 2))
    example_norm = 0.5 * jnp.log(example_sq + 1e-6)
    in_weight_next = in_weight - learn_rate[0] * grad_in
    out_weight_next = out_weight - learn_rate[0] * grad_out
    return (input_grad, in_weight_next, out_weight_next, example_norm)
```

```python
import functools

import jax
import jax.numpy as jnp
from jax import lax
from jax.experimental import pallas as pl
from jax.experimental.pallas import tpu as pltpu
from jax.sharding import Mesh, PartitionSpec as P

D = 6144
FF = 24576
IMAGES = 8
TOK_IMG = 128
TOKENS = 1024
FEAT = 192
NY, NZ, NX = 4, 8, 4
HID = 768
SCALE_IN = D ** (-0.5)
SCALE_OUT = FF ** (-0.5)
NORM_ROWS = 16

root_half = 0.7071067811865476
inv_root_tau = 0.3989422804014327

f32 = jnp.float32
bf16 = jnp.bfloat16
BIG = pltpu.CompilerParams(vmem_limit_bytes=48 * 1024 * 1024)


def dot(left, right, dims):
    return lax.dot_general(left, right, (dims, ((), ())), preferred_element_type=f32)


def split_hidden(weight):
    def body(w_ref, o_ref):
        o_ref[0] = w_ref[...].astype(bf16)

    return pl.pallas_call(
        body,
        grid=(NY,),
        in_specs=[pl.BlockSpec((FEAT, HID), lambda i: (0, i))],
        out_specs=pl.BlockSpec((1, FEAT, HID), lambda i: (i, 0, 0)),
        out_shape=jax.ShapeDtypeStruct((NY, FEAT, HID), bf16),
        compiler_params=BIG,
    )(weight)


def sort_and_project(own, other, order, weight, scale):
    def body(own_ref, oth_ref, p_ref, w_ref, x_ref, part_ref, acc):
        step = pl.program_id(0)
        pieces = [own_ref[0, i] for i in range(NX)] + [oth_ref[0, i] for i in range(NX)]
        rows = jnp.concatenate(pieces, axis=1)
        ordered = dot(rows, p_ref[...], ((1,), (0,))).astype(bf16)
        x_ref[...] = ordered
        prod = dot(ordered, w_ref[0], ((0,), (0,)))

        @pl.when(step == 0)
        def _():
            acc[...] = prod

        @pl.when(step > 0)
        def _():
            acc[...] += prod

        @pl.when(step == NY - 1)
        def _():
            part_ref[...] = (acc[...] * scale).astype(bf16)

    return pl.pallas_call(
        body,
        grid=(NY,),
        in_specs=[
            pl.BlockSpec((1, NX, FEAT, 128), lambda i: (i, 0, 0, 0)),
            pl.BlockSpec((1, NX, FEAT, 128), lambda i: (i, 0, 0, 0)),
            pl.BlockSpec((TOKENS, TOKENS), lambda i: (0, 0)),
            pl.BlockSpec((1, FEAT, HID), lambda i: (i, 0, 0)),
        ],
        out_specs=[
            pl.BlockSpec((FEAT, TOKENS), lambda i: (i, 0)),
            pl.BlockSpec((TOKENS, HID), lambda i: (0, 0)),
        ],
        out_shape=[
            jax.ShapeDtypeStruct((NY * FEAT, TOKENS), bf16),
            jax.ShapeDtypeStruct((TOKENS, HID), bf16),
        ],
        scratch_shapes=[pltpu.VMEM((TOKENS, HID), f32)],
        compiler_params=BIG,
    )(own, other, order, weight)


def image_grads(feats, hidden, scale):
    tile = 256

    def body(x_ref, h_ref, g_ref, sq_ref):
        step = pl.program_id(0)
        total = None
        sums = []
        for b in range(IMAGES):
            block = dot(
                x_ref[:, b * TOK_IMG : (b + 1) * TOK_IMG],
                h_ref[b * TOK_IMG : (b + 1) * TOK_IMG, :],
                ((1,), (0,)),
            )
            total = block if total is None else total + block
            squares = jnp.sum(block * block, axis=0, keepdims=True)
            lanes = squares[:, 0:128]
            for j in range(1, HID // 128):
                lanes = lanes + squares[:, j * 128 : (j + 1) * 128]
            sums.append(lanes)
        g_ref[...] = (total * scale).astype(bf16)
        found = jnp.concatenate(sums, axis=0) * (scale * scale)

        @pl.when(step == 0)
        def _():
            sq_ref[...] = found

        @pl.when(step > 0)
        def _():
            sq_ref[...] += found

    rows = NY * FEAT
    return pl.pallas_call(
        body,
        grid=(rows // tile,),
        in_specs=[
            pl.BlockSpec((tile, TOKENS), lambda i: (i, 0)),
            pl.BlockSpec((TOKENS, HID), lambda i: (0, 0)),
        ],
        out_specs=[
            pl.BlockSpec((tile, HID), lambda i: (i, 0)),
            pl.BlockSpec((IMAGES, 128), lambda i: (0, 0)),
        ],
        out_shape=[
            jax.ShapeDtypeStruct((rows, HID), bf16),
            jax.ShapeDtypeStruct((IMAGES, 128), f32),
        ],
        compiler_params=BIG,
    )(feats, hidden)


def input_grads(weight, hidden, order, norms):
    def body(w_ref, h_ref, p_ref, n_ref, o_ref):
        grad = (dot(w_ref[0], h_ref[...], ((1,), (1,))) * SCALE_IN).astype(bf16)
        placed = dot(grad, p_ref[...], ((1,), (1,))).astype(bf16)
        for core in range(2):
            for i in range(NX):
                at = (core * NX + i) * 128
                o_ref[core, 0, i, 0:FEAT, :] = placed[:, at : at + 128]
                o_ref[core, 0, i, FEAT:, :] = n_ref[...]

    rows = FEAT + NORM_ROWS
    return pl.pallas_call(
        body,
        grid=(NY,),
        in_specs=[
            pl.BlockSpec((1, FEAT, HID), lambda i: (i, 0, 0)),
            pl.BlockSpec((TOKENS, HID), lambda i: (0, 0)),
            pl.BlockSpec((TOKENS, TOKENS), lambda i: (0, 0)),
            pl.BlockSpec((NORM_ROWS, 128), lambda i: (0, 0)),
        ],
        out_specs=pl.BlockSpec((2, 1, NX, rows, 128), lambda i: (0, i, 0, 0, 0)),
        out_shape=jax.ShapeDtypeStruct((2, NY, NX, rows, 128), bf16),
        compiler_params=BIG,
    )(weight, hidden, order, norms)


def update(weight, grads, rate):
    def body(rate_ref, w_ref, g_ref, o_ref):
        o_ref[...] = w_ref[...] - rate_ref[0] * g_ref[0].astype(f32)

    return pl.pallas_call(
        body,
        grid=(NY,),
        in_specs=[
            pl.BlockSpec(memory_space=pltpu.SMEM),
            pl.BlockSpec((FEAT, HID), lambda i: (0, i)),
            pl.BlockSpec((1, FEAT, HID), lambda i: (i, 0, 0)),
        ],
        out_specs=pl.BlockSpec((FEAT, HID), lambda i: (0, i)),
        out_shape=jax.ShapeDtypeStruct(weight.shape, f32),
        compiler_params=BIG,
    )(rate, weight, grads)


def gelu_and_slope(pre):
    phi = 0.5 * (1.0 + lax.erf(pre * root_half))
    return pre * phi, phi + pre * jnp.exp(-0.5 * pre * pre) * inv_root_tau


def exchange(value, axes):
    return lax.all_to_all(value, axes, 0, 0, tiled=True)


def swap_cores(value):
    return lax.ppermute(value, "core", [(0, 1), (1, 0)])


def gather_yx(feats):
    own = exchange(jnp.broadcast_to(feats, (NY * NX, *feats.shape)), ("y", "x"))
    own = own.reshape(NY, NX, *feats.shape)
    return own, swap_cores(own)


def token_order(image_ids, core):
    at = jnp.arange(TOKENS)
    same = (image_ids[:, None] == image_ids[None, :]) & (at[None, :] < at[:, None])
    place = image_ids * TOK_IMG + jnp.sum(same.astype(jnp.int32), axis=1)
    halves = place.reshape(NX, 2, 128).transpose(1, 0, 2)
    halves = jnp.where(core == 0, halves, halves[::-1])
    return (halves.reshape(TOKENS)[:, None] == at[None, :]).astype(bf16)


def shards(tokens, out_grad, image_ids, learn_rate, in_weight, out_weight):
    core = lax.axis_index("core")
    out_weight_t = out_weight.T
    in_mine = exchange(split_hidden(in_weight).reshape(NY * FEAT, HID), "y").reshape(NY, FEAT, HID)
    out_mine = exchange(split_hidden(out_weight_t).reshape(NY * FEAT, HID), "y").reshape(
        NY, FEAT, HID
    )
    order = token_order(image_ids, core)
    tok_sorted, pre_part = sort_and_project(*gather_yx(tokens.T), order, in_mine, SCALE_IN)
    grad_sorted, grad_part = sort_and_project(*gather_yx(out_grad.T), order, out_mine, SCALE_OUT)
    both = jnp.concatenate(
        [
            pre_part.reshape(NZ, TOK_IMG, HID),
            grad_part.reshape(NZ, TOK_IMG, HID),
        ],
        axis=1,
    )
    summed = lax.psum_scatter(both, "z", scatter_dimension=0).astype(f32)
    pre_act, act_grad = summed[:TOK_IMG], summed[TOK_IMG:]
    act, slope = gelu_and_slope(pre_act)
    mine = jnp.stack([act.astype(bf16), (act_grad * slope).astype(bf16)])
    every = lax.all_gather(mine, "z")
    act_all = every[:, 0].reshape(TOKENS, HID)
    hid_all = every[:, 1].reshape(TOKENS, HID)
    in_sum, in_sq = image_grads(tok_sorted, hid_all, SCALE_IN)
    out_sum, out_sq = image_grads(grad_sorted, act_all, SCALE_OUT)
    squares = jnp.sum(in_sq + out_sq, axis=1)
    high = squares.astype(bf16)
    rest = squares - high.astype(f32)
    middle = rest.astype(bf16)
    low = (rest - middle.astype(f32)).astype(bf16)
    lanes = jnp.arange(128)[None, :]
    triple = jnp.stack([high, middle, low])
    spread = jnp.pad(jnp.tile(triple, (1, 2)), ((0, NORM_ROWS - 3), (0, 128 - 2 * IMAGES)))
    norms = jnp.where(lanes // IMAGES == core, spread, jnp.zeros_like(spread))
    parts = input_grads(in_mine, hid_all, order, norms)
    merged = (parts[0].astype(f32) + swap_cores(parts[1]).astype(f32)).astype(bf16)
    rows = FEAT + NORM_ROWS
    got = exchange(merged.reshape(NY * NX, rows, 128), ("y", "x"))
    got = jnp.sum(got.astype(f32), axis=0)
    input_grad = got[:FEAT].astype(bf16).T
    sq_here = jnp.sum(got[FEAT:], axis=0)
    sq_here = sq_here[:IMAGES] + sq_here[IMAGES : 2 * IMAGES]
    sq_all = exchange(jnp.broadcast_to(sq_here, (NZ, 8, IMAGES)), "z")
    example_sq = jnp.sum(sq_all[:, 0], axis=0)
    example_norm = 0.5 * jnp.log(example_sq + 1e-06)
    in_back = exchange(in_sum, "y").reshape(NY, FEAT, HID)
    out_back = exchange(out_sum, "y").reshape(NY, FEAT, HID)
    in_next = update(in_weight, in_back, learn_rate)
    out_next = update(out_weight_t, out_back, learn_rate).T
    return (input_grad, in_next, out_next, example_norm)


def solution(mesh):
    chips = Mesh(mesh.devices.reshape(NY, NZ, NX, 2), ("y", "z", "x", "core"))
    row, col = ("y", "z"), ("x", "core")
    placed = (P(col, row), P(col, row), P(), P(), P(row, col), P(col, row))
    return jax.shard_map(
        shards,
        mesh=chips,
        in_specs=placed,
        out_specs=(P(col, row), P(row, col), P(col, row), P()),
        check_vma=False,
    )
```

```python
import functools

import jax
import jax.numpy as jnp
from jax import lax
from jax.experimental import pallas as pl
from jax.experimental.pallas import tpu as pltpu
from jax.sharding import Mesh, PartitionSpec as P

D = 6144
FF = 24576
IMAGES = 8
TOK_IMG = 128
TOKENS = 1024
FEAT = 192
NY, NZ, NX = 4, 8, 4
HID = 768
SCALE_IN = D ** (-0.5)
SCALE_OUT = FF ** (-0.5)
NORM_ROWS = 16

root_half = 0.7071067811865476
inv_root_tau = 0.3989422804014327

f32 = jnp.float32
bf16 = jnp.bfloat16
WIDE = HID + TOK_IMG
SENT = 2 * TOK_IMG + NORM_ROWS
BIG = pltpu.CompilerParams(vmem_limit_bytes=40 * 1024 * 1024)
VMEM = pl.BlockSpec(memory_space=pltpu.VMEM)
SMEM = pl.BlockSpec(memory_space=pltpu.SMEM)


def dot(left, right, dims):
    return lax.dot_general(left, right, (dims, ((), ())), preferred_element_type=f32)


def split_hidden(in_weight, out_weight_t):
    def body(a_ref, b_ref, o_ref):
        o_ref[0, 0] = a_ref[...].astype(bf16)
        o_ref[0, 1] = b_ref[...].astype(bf16)

    return pl.pallas_call(
        body,
        grid=(NY,),
        in_specs=[pl.BlockSpec((FEAT, HID), lambda i: (0, i))] * 2,
        out_specs=pl.BlockSpec((1, 2, FEAT, HID), lambda i: (i, 0, 0, 0)),
        out_shape=jax.ShapeDtypeStruct((NY, 2, FEAT, HID), bf16),
        compiler_params=BIG,
    )(in_weight, out_weight_t)


def behind(mine, step, size):
    return lax.rem(mine - step + size, size)


def sort_tokens(here, own, other, order):
    def body(here_ref, *refs):
        pieces, (p_ref, x_ref, t_ref, pair_ref, rows) = refs[:8], refs[8:]
        for s in range(NY):
            at = pl.multiple_of(behind(here_ref[0], s, NY) * FEAT, FEAT)
            for u in range(NX):
                x = behind(here_ref[2], u, NX)
                for o in range(2):
                    core = here_ref[3] if o == 0 else 1 - here_ref[3]
                    lane = pl.multiple_of((x * 2 + core) * 128, 128)
                    for a in range(2):
                        rows[a, pl.ds(at, FEAT), pl.ds(lane, 128)] = pieces[o * NX + u][s, a]
        tile = 2 * TOK_IMG
        for a in range(2):

            def one(t, carry, a=a):
                at = pl.multiple_of(t * tile, tile)
                ordered = dot(rows[a], p_ref[:, pl.ds(at, tile)], ((1,), (0,))).astype(bf16)
                x_ref[a, :, pl.ds(at, tile)] = ordered
                turned = ordered.T
                t_ref[a, pl.ds(at, tile), :] = turned
                for k in range(2):
                    image = slice(k * TOK_IMG, (k + 1) * TOK_IMG)
                    pairs = dot(turned[image], ordered[:, image], ((1,), (0,)))
                    pair_ref[2 * t + k, a * TOK_IMG : (a + 1) * TOK_IMG, :] = pairs.astype(bf16)
                return carry

            lax.fori_loop(0, TOKENS // tile, one, 0)

    return pl.pallas_call(
        body,
        in_specs=[SMEM] + [VMEM] * 9,
        out_specs=[VMEM] * 3,
        out_shape=[
            jax.ShapeDtypeStruct((2, NY * FEAT, TOKENS), bf16),
            jax.ShapeDtypeStruct((2, TOKENS, NY * FEAT), bf16),
            jax.ShapeDtypeStruct((IMAGES, 2 * TOK_IMG, TOK_IMG), bf16),
        ],
        scratch_shapes=[pltpu.VMEM((2, NY * FEAT, TOKENS), bf16)],
        compiler_params=BIG,
    )(here, *own, *other, order)


def project(rows, pairs, weights):
    def body(r_ref, p_ref, w_ref, o_ref):
        tile = 2 * TOK_IMG
        o_ref[:, :, HID:] = p_ref[...]
        for a, scale in enumerate((SCALE_IN, SCALE_OUT)):
            weight = w_ref[:, a].reshape(NY * FEAT, HID)

            def one(t, carry, a=a, scale=scale, weight=weight):
                at = pl.multiple_of(t * tile, tile)
                prod = dot(r_ref[a, pl.ds(at, tile), :], weight, ((1,), (0,)))
                prod = (prod * scale).astype(bf16).reshape(2, TOK_IMG, HID)
                o_ref[pl.ds(2 * t, 2), a * TOK_IMG : (a + 1) * TOK_IMG, 0:HID] = prod
                return carry

            lax.fori_loop(0, TOKENS // tile, one, 0)

    return pl.pallas_call(
        body,
        in_specs=[VMEM] * 3,
        out_specs=VMEM,
        out_shape=jax.ShapeDtypeStruct((IMAGES, 2 * TOK_IMG, WIDE), bf16),
        compiler_params=BIG,
    )(rows, pairs, weights)


def activate(here, summed):
    def body(here_ref, s_ref, o_ref):
        pre = s_ref[0:TOK_IMG, 0:HID].astype(f32)
        act, slope = gelu_and_slope(pre)
        act = act.astype(bf16)
        hid = (s_ref[TOK_IMG:, 0:HID].astype(f32) * slope).astype(bf16)
        o_ref[0:TOK_IMG, :] = act
        o_ref[TOK_IMG : 2 * TOK_IMG, :] = hid
        pairs = s_ref[:, HID:].astype(f32)
        both = dot(hid, hid, ((1,), (1,))) * pairs[0:TOK_IMG] * (SCALE_IN * SCALE_IN)
        both += dot(act, act, ((1,), (1,))) * pairs[TOK_IMG:] * (SCALE_OUT * SCALE_OUT)
        square = jnp.sum(jnp.sum(both, axis=0, keepdims=True), axis=1, keepdims=True)
        high = square.astype(bf16).astype(f32)
        middle = (square - high).astype(bf16).astype(f32)
        low = square - high - middle
        source = (here_ref[0] * NX + here_ref[2]) * 2 + here_ref[3]
        spot = lax.rem(source, 16) * IMAGES + here_ref[1]
        row = lax.broadcasted_iota(jnp.int32, (NORM_ROWS, 128), 0)
        lane = lax.broadcasted_iota(jnp.int32, (NORM_ROWS, 128), 1)
        kind = row - lax.div(source, 16) * 3
        value = jnp.where(kind == 0, high, jnp.where(kind == 1, middle, low))
        kept = (lane == spot) & (kind >= 0) & (kind < 3)
        o_ref[2 * TOK_IMG :, :] = jnp.zeros((NORM_ROWS, HID), bf16)
        o_ref[2 * TOK_IMG :, 0:128] = jnp.where(kept, value, 0.0).astype(bf16)

    return pl.pallas_call(
        body,
        in_specs=[SMEM, VMEM],
        out_specs=VMEM,
        out_shape=jax.ShapeDtypeStruct((SENT, HID), bf16),
        compiler_params=BIG,
    )(here, summed)


def weight_grads(feats, every):
    def body(x_ref, e_ref, g_ref):
        tile = 256
        for w, scale in enumerate((SCALE_IN, SCALE_OUT)):
            rows = slice((1 - w) * TOK_IMG, (2 - w) * TOK_IMG)
            for n in range(HID // tile):
                cols = slice(n * tile, (n + 1) * tile)
                hidden = e_ref[:, rows, cols].reshape(TOKENS, tile)
                grad = dot(x_ref[w], hidden, ((1,), (0,))) * scale
                g_ref[:, w, :, cols] = grad.astype(bf16).reshape(NY, FEAT, tile)

    return pl.pallas_call(
        body,
        in_specs=[VMEM] * 2,
        out_specs=VMEM,
        out_shape=jax.ShapeDtypeStruct((NY, 2, FEAT, HID), bf16),
        compiler_params=BIG,
    )(feats, every)


def input_grads(here, weights, every, order):
    def body(here_ref, w_ref, e_ref, p_ref, own_ref, oth_ref):
        tile = 2 * TOK_IMG
        hidden = e_ref[:, TOK_IMG : 2 * TOK_IMG, :].reshape(TOKENS, HID)
        weight = w_ref[:, 0].reshape(NY * FEAT, HID)
        norms = e_ref[0, 2 * TOK_IMG :, 0:128].astype(f32)
        for b in range(1, IMAGES):
            norms += e_ref[b, 2 * TOK_IMG :, 0:128].astype(f32)
        norms = norms.astype(bf16)

        def one(x, carry):
            at = pl.multiple_of(x * tile, tile)
            rows = dot(p_ref[pl.ds(at, tile), :], hidden, ((1,), (0,))).astype(bf16)
            grad = (dot(weight, rows, ((1,), (1,))) * SCALE_IN).astype(bf16)
            left, right = grad[:, :128], grad[:, 128:]
            u = lax.rem(x - here_ref[2] + NX, NX)
            for core in range(2):

                @pl.when(here_ref[3] == core)
                def _():
                    halves = (left, right) if core == 0 else (right, left)
                    for ref, half in zip((own_ref, oth_ref), halves):
                        for y in range(NY):
                            v = lax.rem(y - here_ref[0] + NY, NY)
                            ref[u, v, 0:FEAT, :] = half[y * FEAT : (y + 1) * FEAT]
                            ref[u, v, FEAT:, :] = norms

            return carry

        lax.fori_loop(0, NX, one, 0)

    return pl.pallas_call(
        body,
        in_specs=[SMEM] + [VMEM] * 3,
        out_specs=[VMEM] * 2,
        out_shape=[jax.ShapeDtypeStruct((NX, NY, FEAT + NORM_ROWS, 128), bf16)] * 2,
        compiler_params=BIG,
    )(here, weights, every, order)


def update(rate, in_weight, out_weight_t, grads):
    def body(rate_ref, a_ref, b_ref, g_ref, a_out, b_out):
        a_out[...] = a_ref[...] - rate_ref[0] * g_ref[0, 0].astype(f32)
        b_out[...] = b_ref[...] - rate_ref[0] * g_ref[0, 1].astype(f32)

    block = pl.BlockSpec((FEAT, HID), lambda i: (0, i))
    return pl.pallas_call(
        body,
        grid=(NY,),
        in_specs=[
            pl.BlockSpec(memory_space=pltpu.SMEM),
            block,
            block,
            pl.BlockSpec((1, 2, FEAT, HID), lambda i: (i, 0, 0, 0)),
        ],
        out_specs=[block, block],
        out_shape=[jax.ShapeDtypeStruct(in_weight.shape, f32)] * 2,
        compiler_params=BIG,
    )(rate, in_weight, out_weight_t, grads)


def behind(mine, step, size):
    return lax.rem(mine - step + size, size)


def gelu_and_slope(pre):
    phi = 0.5 * (1.0 + lax.erf(pre * root_half))
    return pre * phi, phi + pre * jnp.exp(-0.5 * pre * pre) * inv_root_tau


def exchange(value, axes):
    return lax.all_to_all(value, axes, 0, 0, tiled=True)


def swap_cores(value):
    return lax.ppermute(value, "core", [(0, 1), (1, 0)])


def ahead(value, axis, step):
    return lax.ppermute(value, axis, [(i, (i + step) % 4) for i in range(4)])


def ring_gather(value, axis):
    near, back, far = ahead(value, axis, 1), ahead(value, axis, 3), ahead(value, axis, 2)
    return [value, near, far, back]


def token_order(image_ids):
    at = jnp.arange(TOKENS)
    same = (image_ids[:, None] == image_ids[None, :]) & (at[None, :] < at[:, None])
    place = image_ids * TOK_IMG + jnp.sum(same.astype(jnp.int32), axis=1)
    return (place[:, None] == at[None, :]).astype(bf16)


def ring_sum(chunks, axis):
    total = chunks[0].astype(f32)
    for s in (1, 3, 2):
        total += ahead(chunks[s], axis, s).astype(f32)
    return total


def shards(tokens, out_grad, image_ids, learn_rate, in_weight, out_weight):
    here = jnp.stack([lax.axis_index(a) for a in ("y", "z", "x", "core")]).astype(jnp.int32)
    out_weight_t = out_weight.T
    halves = split_hidden(in_weight, out_weight_t)
    along_y = jnp.stack(ring_gather(jnp.stack([tokens.T, out_grad.T]), "y"))
    halves, along_y = lax.optimization_barrier((halves, along_y))
    weights = exchange(halves.reshape(NY * 2 * FEAT, HID), "y").reshape(NY, 2, FEAT, HID)
    own = ring_gather(along_y, "x")
    other = [swap_cores(piece) for piece in own]
    order = token_order(image_ids)
    feats, rows, pairs = sort_tokens(here, own, other, order)
    parts = project(rows, pairs, weights)
    summed = lax.psum_scatter(parts, "z", scatter_dimension=0)
    every = lax.all_gather(activate(here, summed), "z")
    grads = weight_grads(feats, every)
    mine, theirs = input_grads(here, weights, every, order)
    grads = exchange(grads.reshape(NY * 2 * FEAT, HID), "y").reshape(NY, 2, FEAT, HID)
    merged = (mine.astype(f32) + swap_cores(theirs).astype(f32)).astype(bf16)
    along_x = ring_sum(merged, "x").astype(bf16)
    got = ring_sum(along_x, "y")
    input_grad = got[:FEAT].astype(bf16).T
    example_sq = jnp.sum(got[FEAT:].reshape(NORM_ROWS * 16, IMAGES), axis=0)
    example_norm = 0.5 * jnp.log(example_sq + 1e-06)
    in_next, out_next = update(learn_rate, in_weight, out_weight_t, grads)
    return (input_grad, in_next, out_next.T, example_norm)


def solution(mesh):
    chips = Mesh(mesh.devices.reshape(NY, NZ, NX, 2), ("y", "z", "x", "core"))
    row, col = ("y", "z"), ("x", "core")
    placed = (P(col, row), P(col, row), P(), P(), P(row, col), P(col, row))
    return jax.shard_map(
        shards,
        mesh=chips,
        in_specs=placed,
        out_specs=(P(col, row), P(row, col), P(col, row), P()),
        check_vma=False,
    )
```

```python
import functools

import jax
import jax.numpy as jnp
from jax import lax
from jax.experimental import pallas as pl
from jax.experimental.pallas import tpu as pltpu
from jax.sharding import Mesh, PartitionSpec as P

D = 6144
FF = 24576
IMAGES = 8
TOK_IMG = 128
TOKENS = 1024
FEAT = 192
NY, NZ, NX = 4, 8, 4
HID = 768
SCALE_IN = D ** (-0.5)
SCALE_OUT = FF ** (-0.5)
NORM_ROWS = 16

root_half = 0.7071067811865476
inv_root_tau = 0.3989422804014327

f32 = jnp.float32
bf16 = jnp.bfloat16
WIDE = HID + TOK_IMG
SENT = 2 * TOK_IMG + NORM_ROWS
MIB = 1024 * 1024
SMALL = pltpu.CompilerParams(vmem_limit_bytes=8 * MIB)
MIDDLE = pltpu.CompilerParams(vmem_limit_bytes=24 * MIB)
WHOLE = pltpu.CompilerParams(vmem_limit_bytes=56 * MIB)
VMEM = pl.BlockSpec(memory_space=pltpu.VMEM)
SMEM = pl.BlockSpec(memory_space=pltpu.SMEM)
HBM = pl.BlockSpec(memory_space=pltpu.HBM)
ANY = pl.BlockSpec(memory_space=pl.ANY)
TILE = 4 * TOK_IMG
TILES = TOKENS // TILE
PAIR = 2 * TOK_IMG


def dot(left, right, dims):
    return lax.dot_general(left, right, (dims, ((), ())), preferred_element_type=f32)


def in_hbm(value):
    return pltpu.with_memory_space_constraint(value, pltpu.HBM)


def split_hidden(in_weight, out_weight_t):
    def body(a_ref, b_ref, o_ref):
        o_ref[0, 0] = a_ref[...].astype(bf16)
        o_ref[0, 1] = b_ref[...].astype(bf16)

    return pl.pallas_call(
        body,
        grid=(NY,),
        in_specs=[pl.BlockSpec((FEAT, HID), lambda i: (0, i))] * 2,
        out_specs=pl.BlockSpec((1, 2, FEAT, HID), lambda i: (i, 0, 0, 0)),
        out_shape=pltpu.HBM((NY, 2, FEAT, HID), bf16),
        compiler_params=MIDDLE,
    )(in_hbm(in_weight), in_hbm(out_weight_t))


def fill_order(place_ref, order_ref):
    def one(r, carry):
        at = pl.ds(pl.multiple_of(r * PAIR, PAIR), PAIR)
        place = jnp.concatenate([place_ref[at, :]] * (TOKENS // 128), axis=1)
        column = lax.broadcasted_iota(jnp.int32, (PAIR, TOKENS), 1)
        order_ref[at, :] = jnp.where(place == column, 1.0, 0.0).astype(bf16)
        return carry

    lax.fori_loop(0, TOKENS // PAIR, one, 0)


def behind(mine, step, size):
    return lax.rem(mine - step + size, size)


def sort_tokens(here, own, other, place):
    def body(here_ref, *refs):
        pieces, (p_ref, x_ref, t_ref, pair_ref) = refs[:8], refs[8:12]
        rows, place_buf, p_buf, x_buf, t_buf, pair_buf, in_sem, p_sem, x_sem, t_sem, pair_sem = refs[12:]

        def load(piece):
            o, u = divmod(piece, NX)
            core = here_ref[3] if o == 0 else 1 - here_ref[3]
            lane = pl.multiple_of((behind(here_ref[2], u, NX) * 2 + core) * 128, 128)
            return pltpu.make_async_copy(
                pieces[piece], rows.at[:, :, :, pl.ds(lane, 128)], in_sem.at[piece]
            )

        def stores(a, t):
            at = pl.ds(pl.multiple_of(t * TILE, TILE), TILE)
            return (
                pltpu.make_async_copy(x_buf.at[a, :, at], x_ref.at[a, :, at], x_sem.at[a, t]),
                pltpu.make_async_copy(t_buf.at[a, at], t_ref.at[a, at], t_sem.at[a, t]),
            )

        p_load = pltpu.make_async_copy(p_ref, place_buf, p_sem)
        pair_store = pltpu.make_async_copy(pair_buf, pair_ref, pair_sem)
        loads = [load(piece) for piece in range(8)]
        p_load.start()
        for copy in loads:
            copy.start()
        p_load.wait()
        fill_order(place_buf, p_buf)
        for copy in loads:
            copy.wait()

        def one(i, carry):
            a, t = lax.div(i, TILES), lax.rem(i, TILES)
            at = pl.ds(pl.multiple_of(t * TILE, TILE), TILE)
            given = rows[:, a].reshape(NY * FEAT, TOKENS)
            ordered = dot(given, p_buf[:, at], ((1,), (0,))).astype(bf16)
            x_buf[a, :, at] = ordered
            turned = ordered.T
            t_buf[a, at, :] = turned
            for k in range(4):
                image = slice(k * TOK_IMG, (k + 1) * TOK_IMG)
                pairs = dot(turned[image], ordered[:, image], ((1,), (0,)))
                pair_buf[4 * t + k, a] = pairs.astype(bf16)
            for copy in stores(a, t):
                copy.start()
            return carry

        def finish(i, carry):
            for copy in stores(lax.div(i, TILES), lax.rem(i, TILES)):
                copy.wait()
            return carry

        lax.fori_loop(0, 2 * TILES, one, 0)
        pair_store.start()
        lax.fori_loop(0, 2 * TILES, finish, 0)
        pair_store.wait()

    feats, rows = (2, NY * FEAT, TOKENS), (2, TOKENS, NY * FEAT)
    pairs = (IMAGES, 2, TOK_IMG, TOK_IMG)
    return pl.pallas_call(
        body,
        in_specs=[SMEM] + [HBM] * 9,
        out_specs=[HBM] * 3,
        out_shape=[pltpu.HBM(shape, bf16) for shape in (feats, rows, pairs)],
        scratch_shapes=[
            pltpu.VMEM((NY, 2, FEAT, TOKENS), bf16),
            pltpu.VMEM((TOKENS, 128), jnp.int32),
            pltpu.VMEM((TOKENS, TOKENS), bf16),
            pltpu.VMEM(feats, bf16),
            pltpu.VMEM(rows, bf16),
            pltpu.VMEM(pairs, bf16),
            pltpu.SemaphoreType.DMA((8,)),
            pltpu.SemaphoreType.DMA,
            pltpu.SemaphoreType.DMA((2, TILES)),
            pltpu.SemaphoreType.DMA((2, TILES)),
            pltpu.SemaphoreType.DMA,
        ],
        compiler_params=MIDDLE,
    )(here, *map(in_hbm, (*own, *other, place)))


def project(here, rows, pairs, weights):
    def body(here_ref, r_ref, p_ref, w_ref, o_ref, r_buf, w_buf, o_buf, r_sem, w_sem, p_sem, o_sem):
        w_loads = [
            pltpu.make_async_copy(
                w_ref.at[behind(here_ref[0], s, NY)], w_buf.at[:, s], w_sem.at[s]
            )
            for s in range(NY)
        ]
        p_load = pltpu.make_async_copy(p_ref, o_buf.at[:, :, :, pl.ds(HID, TOK_IMG)], p_sem)

        def load(a):
            return pltpu.make_async_copy(r_ref.at[a], r_buf.at[a], r_sem.at[a])

        def store(a, t):
            part = (pl.ds(4 * t, 4), a)
            return pltpu.make_async_copy(o_buf.at[part], o_ref.at[part], o_sem.at[a, t])

        for copy in w_loads:
            copy.start()
        load(0).start()
        p_load.start()
        load(1).start()
        for copy in w_loads:
            copy.wait()
        load(0).wait()
        p_load.wait()

        def one(i, carry):
            a, t = lax.div(i, TILES), lax.rem(i, TILES)

            @pl.when(i == TILES)
            def _():
                load(1).wait()

            at = pl.ds(pl.multiple_of(t * TILE, TILE), TILE)
            weight = w_buf[a].reshape(NY * FEAT, HID)
            scale = jnp.where(a == 0, f32(SCALE_IN), f32(SCALE_OUT))
            prod = dot(r_buf[a, at, :], weight, ((1,), (0,)))
            prod = (prod * scale).astype(bf16).reshape(4, TOK_IMG, HID)
            o_buf[pl.ds(4 * t, 4), a, :, 0:HID] = prod
            store(a, t).start()
            return carry

        def finish(i, carry):
            store(lax.div(i, TILES), lax.rem(i, TILES)).wait()
            return carry

        lax.fori_loop(0, 2 * TILES, one, 0)
        lax.fori_loop(0, 2 * TILES, finish, 0)

    given = (IMAGES, 2, TOK_IMG, WIDE)
    return pl.pallas_call(
        body,
        in_specs=[SMEM, HBM, HBM, ANY],
        out_specs=HBM,
        out_shape=pltpu.HBM(given, bf16),
        scratch_shapes=[
            pltpu.VMEM((2, TOKENS, NY * FEAT), bf16),
            pltpu.VMEM((2, NY, FEAT, HID), bf16),
            pltpu.VMEM(given, bf16),
            pltpu.SemaphoreType.DMA((2,)),
            pltpu.SemaphoreType.DMA((NY,)),
            pltpu.SemaphoreType.DMA,
            pltpu.SemaphoreType.DMA((2, TILES)),
        ],
        compiler_params=MIDDLE,
    )(here, in_hbm(rows), in_hbm(pairs), weights)


def activate(here, summed):
    def body(here_ref, s_ref, o_ref):
        pre = s_ref[0:TOK_IMG, 0:HID].astype(f32)
        act, slope = gelu_and_slope(pre)
        act = act.astype(bf16)
        hid = (s_ref[TOK_IMG:, 0:HID].astype(f32) * slope).astype(bf16)
        o_ref[0:TOK_IMG, :] = act
        o_ref[TOK_IMG : 2 * TOK_IMG, :] = hid
        pairs = s_ref[:, HID:].astype(f32)
        both = dot(hid, hid, ((1,), (1,))) * pairs[0:TOK_IMG] * (SCALE_IN * SCALE_IN)
        both += dot(act, act, ((1,), (1,))) * pairs[TOK_IMG:] * (SCALE_OUT * SCALE_OUT)
        square = jnp.sum(jnp.sum(both, axis=0, keepdims=True), axis=1, keepdims=True)
        high = square.astype(bf16).astype(f32)
        middle = (square - high).astype(bf16).astype(f32)
        low = square - high - middle
        source = (here_ref[0] * NX + here_ref[2]) * 2 + here_ref[3]
        spot = lax.rem(source, 16) * IMAGES + here_ref[1]
        row = lax.broadcasted_iota(jnp.int32, (NORM_ROWS, 128), 0)
        lane = lax.broadcasted_iota(jnp.int32, (NORM_ROWS, 128), 1)
        kind = row - lax.div(source, 16) * 3
        value = jnp.where(kind == 0, high, jnp.where(kind == 1, middle, low))
        kept = (lane == spot) & (kind >= 0) & (kind < 3)
        o_ref[2 * TOK_IMG :, :] = jnp.zeros((NORM_ROWS, HID), bf16)
        o_ref[2 * TOK_IMG :, 0:128] = jnp.where(kept, value, 0.0).astype(bf16)

    return pl.pallas_call(
        body,
        in_specs=[SMEM, VMEM],
        out_specs=VMEM,
        out_shape=jax.ShapeDtypeStruct((SENT, HID), bf16),
        compiler_params=SMALL,
    )(here, summed)


def all_grads(here, weights, feats, every, place):
    rows = FEAT + NORM_ROWS

    def body(here_ref, w_ref, x_ref, e_ref, p_ref, g_ref, own_ref, oth_ref, *refs):
        w_buf, x_buf, e_buf, n_buf, place_buf, p_buf, g_buf, o_buf = refs[:8]
        w_sem, x_sem, e_sem, n_sem, p_sem, g_sem, o_sem = refs[8:]
        w_load = pltpu.make_async_copy(w_ref.at[:, 0], w_buf, w_sem)
        n_load = pltpu.make_async_copy(
            e_ref.at[:, pl.ds(2 * TOK_IMG, NORM_ROWS), pl.ds(0, 128)], n_buf, n_sem
        )

        def e_load(w):
            part = pl.ds((1 - w) * TOK_IMG, TOK_IMG)
            return pltpu.make_async_copy(e_ref.at[:, part], e_buf.at[w], e_sem.at[w])

        def x_load(w):
            return pltpu.make_async_copy(x_ref.at[w], x_buf.at[w], x_sem.at[w])

        def g_stores(w):
            for s in range(NY):
                y = behind(here_ref[0], s, NY)
                yield pltpu.make_async_copy(g_buf.at[w, s], g_ref.at[y, w], g_sem.at[w, s])

        def stores(x):
            u = lax.rem(x - here_ref[2] + NX, NX)
            yield pltpu.make_async_copy(o_buf.at[1, u], oth_ref.at[u], o_sem.at[1, x])
            yield pltpu.make_async_copy(o_buf.at[0, u], own_ref.at[u], o_sem.at[0, x])

        p_load = pltpu.make_async_copy(p_ref, place_buf, p_sem)
        p_load.start()
        e_load(0).start()
        w_load.start()
        n_load.start()
        x_load(0).start()
        e_load(1).start()
        x_load(1).start()
        p_load.wait()
        fill_order(place_buf, p_buf)
        n_load.wait()
        norms = n_buf[0].astype(f32)
        for b in range(1, IMAGES):
            norms += n_buf[b].astype(f32)
        norms = norms.astype(bf16)
        e_load(0).wait()
        w_load.wait()

        def one(x, carry):
            at = pl.multiple_of(x * PAIR, PAIR)
            hidden = e_buf[0].reshape(TOKENS, HID)
            placed = dot(p_buf[pl.ds(at, PAIR), :], hidden, ((1,), (0,))).astype(bf16)
            weight = w_buf[...].reshape(NY * FEAT, HID)
            grad = (dot(weight, placed, ((1,), (1,))) * SCALE_IN).astype(bf16)
            u = lax.rem(x - here_ref[2] + NX, NX)
            for core in range(2):
                o = lax.rem(core + here_ref[3], 2)
                half = grad[:, core * 128 : (core + 1) * 128]
                for y in range(NY):
                    v = lax.rem(y - here_ref[0] + NY, NY)
                    o_buf[o, u, v, 0:FEAT, :] = half[y * FEAT : (y + 1) * FEAT]
                    o_buf[o, u, v, FEAT:, :] = norms
            for copy in stores(x):
                copy.start()
            return carry

        lax.fori_loop(0, NX, one, 0)
        tile = 256
        steps = HID // tile

        def two(i, carry):
            w, n = lax.div(i, steps), lax.rem(i, steps)

            @pl.when(n == 0)
            def _():
                x_load(w).wait()

            @pl.when(i == steps)
            def _():
                e_load(w).wait()

            cols = pl.ds(pl.multiple_of(n * tile, tile), tile)
            hidden = e_buf[w, :, :, cols].reshape(TOKENS, tile)
            scale = jnp.where(w == 0, f32(SCALE_IN), f32(SCALE_OUT))
            grad = dot(x_buf[w], hidden, ((1,), (0,))) * scale
            g_buf[w, :, :, cols] = grad.astype(bf16).reshape(NY, FEAT, tile)

            @pl.when(n == steps - 1)
            def _():
                for copy in g_stores(w):
                    copy.start()

            return carry

        lax.fori_loop(0, 2 * steps, two, 0)
        for x in range(NX):
            for copy in stores(x):
                copy.wait()
        for w in range(2):
            for copy in g_stores(w):
                copy.wait()

    sums = (NX, NY, rows, 128)
    grads = (NY, 2, FEAT, HID)
    return pl.pallas_call(
        body,
        in_specs=[SMEM] + [HBM] * 4,
        out_specs=[HBM] * 3,
        out_shape=[pltpu.HBM(shape, bf16) for shape in (grads, sums, sums)],
        scratch_shapes=[
            pltpu.VMEM((NY, FEAT, HID), bf16),
            pltpu.VMEM((2, NY * FEAT, TOKENS), bf16),
            pltpu.VMEM((2, IMAGES, TOK_IMG, HID), bf16),
            pltpu.VMEM((IMAGES, NORM_ROWS, 128), bf16),
            pltpu.VMEM((TOKENS, 128), jnp.int32),
            pltpu.VMEM((TOKENS, TOKENS), bf16),
            pltpu.VMEM((2, NY, FEAT, HID), bf16),
            pltpu.VMEM((2, *sums), bf16),
            pltpu.SemaphoreType.DMA,
            pltpu.SemaphoreType.DMA((2,)),
            pltpu.SemaphoreType.DMA((2,)),
            pltpu.SemaphoreType.DMA,
            pltpu.SemaphoreType.DMA,
            pltpu.SemaphoreType.DMA((2, NY)),
            pltpu.SemaphoreType.DMA((2, NX)),
        ],
        compiler_params=MIDDLE,
    )(here, *map(in_hbm, (weights, feats, every, place)))


def update(rate, in_weight, out_weight_t, grads):
    def body(rate_ref, a_ref, b_ref, g_ref, a_out, b_out, w_buf, g_buf, w_sem, g_sem, o_sem):
        def loads(y):
            cols = pl.ds(pl.multiple_of(y * HID, HID), HID)
            return (
                pltpu.make_async_copy(g_ref.at[y], g_buf.at[y], g_sem.at[y]),
                pltpu.make_async_copy(a_ref.at[:, cols], w_buf.at[0, y], w_sem.at[0, y]),
                pltpu.make_async_copy(b_ref.at[:, cols], w_buf.at[1, y], w_sem.at[1, y]),
            )

        def stores(y):
            cols = pl.ds(pl.multiple_of(y * HID, HID), HID)
            return (
                pltpu.make_async_copy(w_buf.at[0, y], a_out.at[:, cols], o_sem.at[0, y]),
                pltpu.make_async_copy(w_buf.at[1, y], b_out.at[:, cols], o_sem.at[1, y]),
            )

        def begin(y, carry):
            for copy in loads(y):
                copy.start()
            return carry

        def one(y, carry):
            for copy in loads(y):
                copy.wait()
            for w in range(2):
                w_buf[w, y] = w_buf[w, y] - rate_ref[0] * g_buf[y, w].astype(f32)
            for copy in stores(y):
                copy.start()
            return carry

        def finish(y, carry):
            for copy in stores(y):
                copy.wait()
            return carry

        lax.fori_loop(0, NY, begin, 0)
        lax.fori_loop(0, NY, one, 0)
        lax.fori_loop(0, NY, finish, 0)

    return pl.pallas_call(
        body,
        in_specs=[SMEM, HBM, HBM, ANY],
        out_specs=[HBM] * 2,
        out_shape=[pltpu.HBM(in_weight.shape, f32)] * 2,
        scratch_shapes=[
            pltpu.VMEM((2, NY, FEAT, HID), f32),
            pltpu.VMEM((NY, 2, FEAT, HID), bf16),
            pltpu.SemaphoreType.DMA((2, NY)),
            pltpu.SemaphoreType.DMA((NY,)),
            pltpu.SemaphoreType.DMA((2, NY)),
        ],
        compiler_params=MIDDLE,
    )(rate, in_hbm(in_weight), in_hbm(out_weight_t), grads)


def gelu_and_slope(pre):
    phi = 0.5 * (1.0 + lax.erf(pre * root_half))
    return pre * phi, phi + pre * jnp.exp(-0.5 * pre * pre) * inv_root_tau


def exchange(value, axes):
    return lax.all_to_all(value, axes, 0, 0, tiled=True)


def swap_cores(value):
    return lax.ppermute(value, "core", [(0, 1), (1, 0)])


def ahead(value, axis, step):
    return lax.ppermute(value, axis, [(i, (i + step) % 4) for i in range(4)])


def ring_gather(value, axis):
    near, back, far = ahead(value, axis, 1), ahead(value, axis, 3), ahead(value, axis, 2)
    return [value, near, far, back]


def token_place(image_ids):
    at = jnp.arange(TOKENS)
    same = (image_ids[:, None] == image_ids[None, :]) & (at[None, :] < at[:, None])
    place = image_ids * TOK_IMG + jnp.sum(same.astype(jnp.int32), axis=1)
    return jnp.broadcast_to(place[:, None], (TOKENS, 128))


def ring_sum(chunks, axis):
    total = chunks[0].astype(f32)
    for s in (1, 3, 2):
        total += ahead(chunks[s], axis, s).astype(f32)
    return total


def shards(tokens, out_grad, image_ids, learn_rate, in_weight, out_weight):
    here = jnp.stack([lax.axis_index(a) for a in ("y", "z", "x", "core")]).astype(jnp.int32)
    out_weight_t = out_weight.T
    halves = split_hidden(in_weight, out_weight_t)
    along_y = jnp.stack(ring_gather(jnp.stack([tokens.T, out_grad.T]), "y"))
    halves, along_y = lax.optimization_barrier((halves, along_y))
    weights = exchange(halves.reshape(NY * 2 * FEAT, HID), "y").reshape(NY, 2, FEAT, HID)
    own = ring_gather(along_y, "x")
    place, own[1] = lax.optimization_barrier((token_place(image_ids), own[1]))
    other = [swap_cores(piece) for piece in own]
    feats, rows, pairs = sort_tokens(here, own, other, place)
    parts = project(here, rows, pairs, weights).reshape(IMAGES, 2 * TOK_IMG, WIDE)
    summed = lax.psum_scatter(parts, "z", scatter_dimension=0)
    every = lax.all_gather(activate(here, summed), "z")
    grads, mine, theirs = all_grads(here, weights, feats, every, place)
    grads = exchange(grads.reshape(NY * 2 * FEAT, HID), "y").reshape(NY, 2, FEAT, HID)
    merged = (mine.astype(f32) + swap_cores(theirs).astype(f32)).astype(bf16)
    along_x = ring_sum(merged, "x").astype(bf16)
    got = ring_sum(along_x, "y")
    input_grad = got[:FEAT].astype(bf16).T
    example_sq = jnp.sum(got[FEAT:].reshape(NORM_ROWS * 16, IMAGES), axis=0)
    example_norm = 0.5 * jnp.log(example_sq + 1e-06)
    in_next, out_next = update(learn_rate, in_weight, out_weight_t, grads)
    return (input_grad, in_next, out_next.T, example_norm)


def solution(mesh):
    chips = Mesh(mesh.devices.reshape(NY, NZ, NX, 2), ("y", "z", "x", "core"))
    row, col = ("y", "z"), ("x", "core")
    placed = (P(col, row), P(col, row), P(), P(), P(row, col), P(col, row))
    return jax.shard_map(
        shards,
        mesh=chips,
        in_specs=placed,
        out_specs=(P(col, row), P(row, col), P(col, row), P()),
        check_vma=False,
    )
```

```python
import functools

import jax
import jax.numpy as jnp
from jax import lax
from jax.experimental import pallas as pl
from jax.experimental.pallas import tpu as pltpu
from jax.sharding import Mesh, PartitionSpec as P

D = 6144
FF = 24576
IMAGES = 8
TOK_IMG = 128
TOKENS = 1024
FEAT = 192
NY, NZ, NX = 4, 8, 4
HID = 768
SCALE_IN = D ** (-0.5)
SCALE_OUT = FF ** (-0.5)
NORM_ROWS = 16
PAIR_ROWS = 2 * TOK_IMG // 8

root_half = 0.7071067811865476
inv_root_tau = 0.3989422804014327

f32 = jnp.float32
bf16 = jnp.bfloat16
MIB = 1024 * 1024
SMALL = pltpu.CompilerParams(vmem_limit_bytes=8 * MIB)
MIDDLE = pltpu.CompilerParams(vmem_limit_bytes=24 * MIB)
WHOLE = pltpu.CompilerParams(vmem_limit_bytes=56 * MIB)
VMEM = pl.BlockSpec(memory_space=pltpu.VMEM)
SMEM = pl.BlockSpec(memory_space=pltpu.SMEM)
HBM = pl.BlockSpec(memory_space=pltpu.HBM)
ANY = pl.BlockSpec(memory_space=pl.ANY)
TILE = 4 * TOK_IMG
TILES = TOKENS // TILE
PAIR = 2 * TOK_IMG


def dot(left, right, dims):
    return lax.dot_general(left, right, (dims, ((), ())), preferred_element_type=f32)


def in_hbm(value):
    return pltpu.with_memory_space_constraint(value, pltpu.HBM)


def split_hidden(in_weight, out_weight_t):
    def body(a_ref, b_ref, o_ref):
        o_ref[0, 0] = a_ref[...].astype(bf16)
        o_ref[0, 1] = b_ref[...].astype(bf16)

    return pl.pallas_call(
        body,
        grid=(NY,),
        in_specs=[pl.BlockSpec((FEAT, HID), lambda i: (0, i))] * 2,
        out_specs=pl.BlockSpec((1, 2, FEAT, HID), lambda i: (i, 0, 0, 0)),
        out_shape=pltpu.HBM((NY, 2, FEAT, HID), bf16),
        compiler_params=MIDDLE,
    )(in_hbm(in_weight), in_hbm(out_weight_t))


def fill_order(place_ref, order_ref):
    def one(r, carry):
        at = pl.ds(pl.multiple_of(r * PAIR, PAIR), PAIR)
        place = jnp.concatenate([place_ref[at, :]] * (TOKENS // 128), axis=1)
        column = lax.broadcasted_iota(jnp.int32, (PAIR, TOKENS), 1)
        order_ref[at, :] = jnp.where(place == column, 1.0, 0.0).astype(bf16)
        return carry

    lax.fori_loop(0, TOKENS // PAIR, one, 0)


def behind(mine, step, size):
    return lax.rem(mine - step + size, size)


def sort_tokens(here, own, other, place):
    def body(here_ref, *refs):
        pieces, (p_ref, x_ref, t_ref, pair_ref) = refs[:8], refs[8:12]
        rows, place_buf, p_buf, x_buf, t_buf, pair_buf, in_sem, p_sem, x_sem, t_sem, pair_sem = refs[12:]

        def load(piece):
            o, u = divmod(piece, NX)
            core = here_ref[3] if o == 0 else 1 - here_ref[3]
            lane = pl.multiple_of((behind(here_ref[2], u, NX) * 2 + core) * 128, 128)
            return pltpu.make_async_copy(
                pieces[piece], rows.at[:, :, :, pl.ds(lane, 128)], in_sem.at[piece]
            )

        def stores(a, t):
            at = pl.ds(pl.multiple_of(t * TILE, TILE), TILE)
            return (
                pltpu.make_async_copy(x_buf.at[a, :, at], x_ref.at[a, :, at], x_sem.at[a, t]),
                pltpu.make_async_copy(t_buf.at[a, at], t_ref.at[a, at], t_sem.at[a, t]),
            )

        share = here_ref[2] * 2 + here_ref[3]
        pair_array = lax.div(share, 4)
        pair_row = lax.rem(share, 4) * PAIR_ROWS
        p_load = pltpu.make_async_copy(p_ref, place_buf, p_sem)
        pair_store = pltpu.make_async_copy(pair_buf, pair_ref, pair_sem)
        loads = [load(piece) for piece in range(8)]
        p_load.start()
        for copy in loads:
            copy.start()
        p_load.wait()
        fill_order(place_buf, p_buf)
        for copy in loads:
            copy.wait()

        def one(i, carry):
            a, t = lax.div(i, TILES), lax.rem(i, TILES)
            at = pl.ds(pl.multiple_of(t * TILE, TILE), TILE)
            given = rows[:, a].reshape(NY * FEAT, TOKENS)
            ordered = dot(given, p_buf[:, at], ((1,), (0,))).astype(bf16)
            x_buf[a, :, at] = ordered
            t_buf[a, at, :] = ordered.T

            @pl.when(a == pair_array)
            def _():
                for k in range(TILE // TOK_IMG):
                    start = t * TILE + k * TOK_IMG + pair_row
                    some = t_buf[a, pl.ds(pl.multiple_of(start, PAIR_ROWS), PAIR_ROWS), :]
                    image = ordered[:, k * TOK_IMG : (k + 1) * TOK_IMG]
                    pair_buf[TILE // TOK_IMG * t + k] = dot(some, image, ((1,), (0,)))

            for copy in stores(a, t):
                copy.start()
            return carry

        def finish(i, carry):
            for copy in stores(lax.div(i, TILES), lax.rem(i, TILES)):
                copy.wait()
            return carry

        lax.fori_loop(0, 2 * TILES, one, 0)
        pair_store.start()
        lax.fori_loop(0, 2 * TILES, finish, 0)
        pair_store.wait()

    feats, rows = (2, NY * FEAT, TOKENS), (2, TOKENS, NY * FEAT)
    pairs = (IMAGES, PAIR_ROWS, TOK_IMG)
    return pl.pallas_call(
        body,
        in_specs=[SMEM] + [HBM] * 9,
        out_specs=[HBM] * 3,
        out_shape=[pltpu.HBM(feats, bf16), pltpu.HBM(rows, bf16), pltpu.HBM(pairs, f32)],
        scratch_shapes=[
            pltpu.VMEM((NY, 2, FEAT, TOKENS), bf16),
            pltpu.VMEM((TOKENS, 128), jnp.int32),
            pltpu.VMEM((TOKENS, TOKENS), bf16),
            pltpu.VMEM(feats, bf16),
            pltpu.VMEM(rows, bf16),
            pltpu.VMEM(pairs, f32),
            pltpu.SemaphoreType.DMA((8,)),
            pltpu.SemaphoreType.DMA,
            pltpu.SemaphoreType.DMA((2, TILES)),
            pltpu.SemaphoreType.DMA((2, TILES)),
            pltpu.SemaphoreType.DMA,
        ],
        compiler_params=MIDDLE,
    )(here, *map(in_hbm, (*own, *other, place)))


def project(here, rows, weights):
    def body(here_ref, r_ref, w_ref, o_ref, r_buf, w_buf, o_buf, r_sem, w_sem, o_sem):
        w_loads = [
            pltpu.make_async_copy(
                w_ref.at[behind(here_ref[0], s, NY)], w_buf.at[:, s], w_sem.at[s]
            )
            for s in range(NY)
        ]

        def load(a):
            return pltpu.make_async_copy(r_ref.at[a], r_buf.at[a], r_sem.at[a])

        def store(a, t):
            part = (pl.ds(4 * t, 4), a)
            return pltpu.make_async_copy(o_buf.at[part], o_ref.at[part], o_sem.at[a, t])

        for copy in w_loads:
            copy.start()
        load(0).start()
        load(1).start()
        for copy in w_loads:
            copy.wait()
        load(0).wait()

        def one(i, carry):
            a, t = lax.div(i, TILES), lax.rem(i, TILES)

            @pl.when(i == TILES)
            def _():
                load(1).wait()

            at = pl.ds(pl.multiple_of(t * TILE, TILE), TILE)
            weight = w_buf[a].reshape(NY * FEAT, HID)
            scale = jnp.where(a == 0, f32(SCALE_IN), f32(SCALE_OUT))
            prod = dot(r_buf[a, at, :], weight, ((1,), (0,)))
            prod = (prod * scale).astype(bf16).reshape(4, TOK_IMG, HID)
            o_buf[pl.ds(4 * t, 4), a] = prod
            store(a, t).start()
            return carry

        def finish(i, carry):
            store(lax.div(i, TILES), lax.rem(i, TILES)).wait()
            return carry

        lax.fori_loop(0, 2 * TILES, one, 0)
        lax.fori_loop(0, 2 * TILES, finish, 0)

    given = (IMAGES, 2, TOK_IMG, HID)
    return pl.pallas_call(
        body,
        in_specs=[SMEM, HBM, ANY],
        out_specs=HBM,
        out_shape=pltpu.HBM(given, bf16),
        scratch_shapes=[
            pltpu.VMEM((2, TOKENS, NY * FEAT), bf16),
            pltpu.VMEM((2, NY, FEAT, HID), bf16),
            pltpu.VMEM(given, bf16),
            pltpu.SemaphoreType.DMA((2,)),
            pltpu.SemaphoreType.DMA((NY,)),
            pltpu.SemaphoreType.DMA((2, TILES)),
        ],
        compiler_params=MIDDLE,
    )(here, in_hbm(rows), weights)


def activate(here, summed, pairs):
    def body(here_ref, s_ref, p_ref, o_ref, n_ref):
        pre = s_ref[0:TOK_IMG, :].astype(f32)
        act, slope = gelu_and_slope(pre)
        act = act.astype(bf16)
        hid = (s_ref[TOK_IMG:, :].astype(f32) * slope).astype(bf16)
        o_ref[0:TOK_IMG, :] = act
        o_ref[TOK_IMG:, :] = hid
        both = dot(hid, hid, ((1,), (1,))) * p_ref[0:TOK_IMG] * (SCALE_IN * SCALE_IN)
        both += dot(act, act, ((1,), (1,))) * p_ref[TOK_IMG:] * (SCALE_OUT * SCALE_OUT)
        square = jnp.sum(jnp.sum(both, axis=0, keepdims=True), axis=1, keepdims=True)
        high = square.astype(bf16).astype(f32)
        middle = (square - high).astype(bf16).astype(f32)
        low = square - high - middle
        source = (here_ref[0] * NX + here_ref[2]) * 2 + here_ref[3]
        spot = lax.rem(source, 16) * IMAGES + here_ref[1]
        row = lax.broadcasted_iota(jnp.int32, (NORM_ROWS, 128), 0)
        lane = lax.broadcasted_iota(jnp.int32, (NORM_ROWS, 128), 1)
        kind = row - lax.div(source, 16) * 3
        value = jnp.where(kind == 0, high, jnp.where(kind == 1, middle, low))
        kept = (lane == spot) & (kind >= 0) & (kind < 3)
        n_ref[...] = jnp.where(kept, value, 0.0).astype(bf16)

    return pl.pallas_call(
        body,
        in_specs=[SMEM, VMEM, VMEM],
        out_specs=[VMEM, VMEM],
        out_shape=[
            jax.ShapeDtypeStruct((2 * TOK_IMG, HID), bf16),
            jax.ShapeDtypeStruct((NORM_ROWS, 128), bf16),
        ],
        compiler_params=SMALL,
    )(here, summed, pairs)


def all_grads(here, weights, feats, every, norms, place):
    rows = FEAT + NORM_ROWS

    def body(here_ref, w_ref, x_ref, e_ref, n_ref, p_ref, g_ref, own_ref, oth_ref, *refs):
        w_buf, x_buf, e_buf, n_buf, place_buf, p_buf, g_buf, o_buf = refs[:8]
        w_sem, x_sem, e_sem, n_sem, p_sem, g_sem, o_sem = refs[8:]
        w_load = pltpu.make_async_copy(w_ref.at[:, 0], w_buf, w_sem)
        n_load = pltpu.make_async_copy(n_ref, n_buf, n_sem)

        def e_load(w):
            part = pl.ds((1 - w) * TOK_IMG, TOK_IMG)
            return pltpu.make_async_copy(e_ref.at[:, part], e_buf.at[w], e_sem.at[w])

        def x_load(w):
            return pltpu.make_async_copy(x_ref.at[w], x_buf.at[w], x_sem.at[w])

        def g_stores(w):
            for s in range(NY):
                y = behind(here_ref[0], s, NY)
                yield pltpu.make_async_copy(g_buf.at[w, s], g_ref.at[y, w], g_sem.at[w, s])

        def stores(x):
            u = lax.rem(x - here_ref[2] + NX, NX)
            yield pltpu.make_async_copy(o_buf.at[1, u], oth_ref.at[u], o_sem.at[1, x])
            yield pltpu.make_async_copy(o_buf.at[0, u], own_ref.at[u], o_sem.at[0, x])

        p_load = pltpu.make_async_copy(p_ref, place_buf, p_sem)
        p_load.start()
        e_load(0).start()
        w_load.start()
        n_load.start()
        x_load(0).start()
        e_load(1).start()
        x_load(1).start()
        p_load.wait()
        fill_order(place_buf, p_buf)
        n_load.wait()
        norms = n_buf[0].astype(f32)
        for b in range(1, IMAGES):
            norms += n_buf[b].astype(f32)
        norms = norms.astype(bf16)
        e_load(0).wait()
        w_load.wait()

        def one(x, carry):
            at = pl.multiple_of(x * PAIR, PAIR)
            hidden = e_buf[0].reshape(TOKENS, HID)
            placed = dot(p_buf[pl.ds(at, PAIR), :], hidden, ((1,), (0,))).astype(bf16)
            weight = w_buf[...].reshape(NY * FEAT, HID)
            grad = (dot(weight, placed, ((1,), (1,))) * SCALE_IN).astype(bf16)
            u = lax.rem(x - here_ref[2] + NX, NX)
            for core in range(2):
                o = lax.rem(core + here_ref[3], 2)
                half = grad[:, core * 128 : (core + 1) * 128]
                for y in range(NY):
                    v = lax.rem(y - here_ref[0] + NY, NY)
                    o_buf[o, u, v, 0:FEAT, :] = half[y * FEAT : (y + 1) * FEAT]
                    o_buf[o, u, v, FEAT:, :] = norms
            for copy in stores(x):
                copy.start()
            return carry

        lax.fori_loop(0, NX, one, 0)
        tile = 256
        steps = HID // tile

        def two(i, carry):
            w, n = lax.div(i, steps), lax.rem(i, steps)

            @pl.when(n == 0)
            def _():
                x_load(w).wait()

            @pl.when(i == steps)
            def _():
                e_load(w).wait()

            cols = pl.ds(pl.multiple_of(n * tile, tile), tile)
            hidden = e_buf[w, :, :, cols].reshape(TOKENS, tile)
            scale = jnp.where(w == 0, f32(SCALE_IN), f32(SCALE_OUT))
            grad = dot(x_buf[w], hidden, ((1,), (0,))) * scale
            g_buf[w, :, :, cols] = grad.astype(bf16).reshape(NY, FEAT, tile)

            @pl.when(n == steps - 1)
            def _():
                for copy in g_stores(w):
                    copy.start()

            return carry

        lax.fori_loop(0, 2 * steps, two, 0)
        for x in range(NX):
            for copy in stores(x):
                copy.wait()
        for w in range(2):
            for copy in g_stores(w):
                copy.wait()

    sums = (NX, NY, rows, 128)
    grads = (NY, 2, FEAT, HID)
    return pl.pallas_call(
        body,
        in_specs=[SMEM] + [HBM] * 3 + [ANY, HBM],
        out_specs=[HBM] * 3,
        out_shape=[pltpu.HBM(shape, bf16) for shape in (grads, sums, sums)],
        scratch_shapes=[
            pltpu.VMEM((NY, FEAT, HID), bf16),
            pltpu.VMEM((2, NY * FEAT, TOKENS), bf16),
            pltpu.VMEM((2, IMAGES, TOK_IMG, HID), bf16),
            pltpu.VMEM((IMAGES, NORM_ROWS, 128), bf16),
            pltpu.VMEM((TOKENS, 128), jnp.int32),
            pltpu.VMEM((TOKENS, TOKENS), bf16),
            pltpu.VMEM((2, NY, FEAT, HID), bf16),
            pltpu.VMEM((2, *sums), bf16),
            pltpu.SemaphoreType.DMA,
            pltpu.SemaphoreType.DMA((2,)),
            pltpu.SemaphoreType.DMA((2,)),
            pltpu.SemaphoreType.DMA,
            pltpu.SemaphoreType.DMA,
            pltpu.SemaphoreType.DMA((2, NY)),
            pltpu.SemaphoreType.DMA((2, NX)),
        ],
        compiler_params=MIDDLE,
    )(here, in_hbm(weights), in_hbm(feats), in_hbm(every), norms, in_hbm(place))


def update(rate, in_weight, out_weight_t, grads):
    def body(rate_ref, a_ref, b_ref, g_ref, a_out, b_out, w_buf, g_buf, w_sem, g_sem, o_sem):
        def loads(y):
            cols = pl.ds(pl.multiple_of(y * HID, HID), HID)
            return (
                pltpu.make_async_copy(g_ref.at[y], g_buf.at[y], g_sem.at[y]),
                pltpu.make_async_copy(a_ref.at[:, cols], w_buf.at[0, y], w_sem.at[0, y]),
                pltpu.make_async_copy(b_ref.at[:, cols], w_buf.at[1, y], w_sem.at[1, y]),
            )

        def stores(y):
            cols = pl.ds(pl.multiple_of(y * HID, HID), HID)
            return (
                pltpu.make_async_copy(w_buf.at[0, y], a_out.at[:, cols], o_sem.at[0, y]),
                pltpu.make_async_copy(w_buf.at[1, y], b_out.at[:, cols], o_sem.at[1, y]),
            )

        def begin(y, carry):
            for copy in loads(y):
                copy.start()
            return carry

        def one(y, carry):
            for copy in loads(y):
                copy.wait()
            for w in range(2):
                w_buf[w, y] = w_buf[w, y] - rate_ref[0] * g_buf[y, w].astype(f32)
            for copy in stores(y):
                copy.start()
            return carry

        def finish(y, carry):
            for copy in stores(y):
                copy.wait()
            return carry

        lax.fori_loop(0, NY, begin, 0)
        lax.fori_loop(0, NY, one, 0)
        lax.fori_loop(0, NY, finish, 0)

    return pl.pallas_call(
        body,
        in_specs=[SMEM, HBM, HBM, ANY],
        out_specs=[HBM] * 2,
        out_shape=[pltpu.HBM(in_weight.shape, f32)] * 2,
        scratch_shapes=[
            pltpu.VMEM((2, NY, FEAT, HID), f32),
            pltpu.VMEM((NY, 2, FEAT, HID), bf16),
            pltpu.SemaphoreType.DMA((2, NY)),
            pltpu.SemaphoreType.DMA((NY,)),
            pltpu.SemaphoreType.DMA((2, NY)),
        ],
        compiler_params=MIDDLE,
    )(rate, in_hbm(in_weight), in_hbm(out_weight_t), grads)


def gelu_and_slope(pre):
    phi = 0.5 * (1.0 + lax.erf(pre * root_half))
    return pre * phi, phi + pre * jnp.exp(-0.5 * pre * pre) * inv_root_tau


def exchange(value, axes):
    return lax.all_to_all(value, axes, 0, 0, tiled=True)


def swap_cores(value):
    return lax.ppermute(value, "core", [(0, 1), (1, 0)])


def ahead(value, axis, step):
    return lax.ppermute(value, axis, [(i, (i + step) % 4) for i in range(4)])


def ring_gather(value, axis):
    near, back, far = ahead(value, axis, 1), ahead(value, axis, 3), ahead(value, axis, 2)
    return [value, near, far, back]


def token_place(image_ids):
    at = jnp.arange(TOKENS)
    same = (image_ids[:, None] == image_ids[None, :]) & (at[None, :] < at[:, None])
    place = image_ids * TOK_IMG + jnp.sum(same.astype(jnp.int32), axis=1)
    return jnp.broadcast_to(place[:, None], (TOKENS, 128))


def ring_sum(chunks, axis):
    total = chunks[0].astype(f32)
    for s in (1, 3, 2):
        total += ahead(chunks[s], axis, s).astype(f32)
    return total


def shards(tokens, out_grad, image_ids, learn_rate, in_weight, out_weight):
    here = jnp.stack([lax.axis_index(a) for a in ("y", "z", "x", "core")]).astype(jnp.int32)
    out_weight_t = out_weight.T
    halves = split_hidden(in_weight, out_weight_t)
    along_y = jnp.stack(ring_gather(jnp.stack([tokens.T, out_grad.T]), "y"))
    halves, along_y = lax.optimization_barrier((halves, along_y))
    weights = exchange(halves.reshape(NY * 2 * FEAT, HID), "y").reshape(NY, 2, FEAT, HID)
    own = ring_gather(along_y, "x")
    place, own[1] = lax.optimization_barrier((token_place(image_ids), own[1]))
    other = [swap_cores(piece) for piece in own]
    feats, rows, pairs = sort_tokens(here, own, other, place)
    parts = project(here, rows, weights).reshape(IMAGES, 2 * TOK_IMG, HID)
    summed = lax.psum_scatter(parts, "z", scatter_dimension=0)
    pairs = exchange(pairs.reshape(IMAGES * PAIR_ROWS, TOK_IMG), "z")
    pairs = jnp.sum(pairs.reshape(NZ, PAIR_ROWS, TOK_IMG), axis=0)
    pairs = lax.all_gather(pairs, ("x", "core"), axis=0, tiled=True)
    sent, norms = activate(here, summed, pairs)
    every = lax.all_gather(sent, "z")
    norms = exchange(jnp.tile(norms, (NZ, 1)), "z").reshape(NZ, NORM_ROWS, 128)
    grads, mine, theirs = all_grads(here, weights, feats, every, norms, place)
    grads = exchange(grads.reshape(NY * 2 * FEAT, HID), "y").reshape(NY, 2, FEAT, HID)
    merged = (mine.astype(f32) + swap_cores(theirs).astype(f32)).astype(bf16)
    along_x = ring_sum(merged, "x").astype(bf16)
    got = ring_sum(along_x, "y")
    input_grad = got[:FEAT].astype(bf16).T
    example_sq = jnp.sum(got[FEAT:].reshape(NORM_ROWS * 16, IMAGES), axis=0)
    example_norm = 0.5 * jnp.log(example_sq + 1e-06)
    in_next, out_next = update(learn_rate, in_weight, out_weight_t, grads)
    return (input_grad, in_next, out_next.T, example_norm)


def solution(mesh):
    chips = Mesh(mesh.devices.reshape(NY, NZ, NX, 2), ("y", "z", "x", "core"))
    row, col = ("y", "z"), ("x", "core")
    placed = (P(col, row), P(col, row), P(), P(), P(row, col), P(col, row))
    return jax.shard_map(
        shards,
        mesh=chips,
        in_specs=placed,
        out_specs=(P(col, row), P(row, col), P(col, row), P()),
        check_vma=False,
    )
```

```python
import functools

import jax
import jax.numpy as jnp
from jax import lax
from jax.experimental import pallas as pl
from jax.experimental.pallas import tpu as pltpu
from jax.sharding import Mesh, PartitionSpec as P

D = 6144
FF = 24576
IMAGES = 8
TOK_IMG = 128
TOKENS = 1024
FEAT = 192
NY, NZ, NX = 4, 8, 4
HID = 768
SCALE_IN = D ** (-0.5)
SCALE_OUT = FF ** (-0.5)
NORM_ROWS = 16
PAIR_ROWS = 2 * TOK_IMG // 8

root_half = 0.7071067811865476
inv_root_tau = 0.3989422804014327

f32 = jnp.float32
bf16 = jnp.bfloat16
MIB = 1024 * 1024
SMALL = pltpu.CompilerParams(vmem_limit_bytes=8 * MIB)
MIDDLE = pltpu.CompilerParams(vmem_limit_bytes=24 * MIB)
WHOLE = pltpu.CompilerParams(vmem_limit_bytes=56 * MIB)
VMEM = pl.BlockSpec(memory_space=pltpu.VMEM)
SMEM = pl.BlockSpec(memory_space=pltpu.SMEM)
HBM = pl.BlockSpec(memory_space=pltpu.HBM)
ANY = pl.BlockSpec(memory_space=pl.ANY)
TILE = 4 * TOK_IMG
TILES = TOKENS // TILE
PAIR = 2 * TOK_IMG


def dot(left, right, dims):
    return lax.dot_general(left, right, (dims, ((), ())), preferred_element_type=f32)


def in_hbm(value):
    return pltpu.with_memory_space_constraint(value, pltpu.HBM)


def split_hidden(in_weight, out_weight_t):
    def body(a_ref, b_ref, o_ref, w_buf, o_buf, w_sem, o_sem):
        def loads(y):
            cols = pl.ds(pl.multiple_of(y * HID, HID), HID)
            return (
                pltpu.make_async_copy(a_ref.at[:, cols], w_buf.at[0, y], w_sem.at[0, y]),
                pltpu.make_async_copy(b_ref.at[:, cols], w_buf.at[1, y], w_sem.at[1, y]),
            )

        def store(y):
            return pltpu.make_async_copy(o_buf.at[y], o_ref.at[y], o_sem.at[y])

        def begin(y, carry):
            for copy in loads(y):
                copy.start()
            return carry

        def one(y, carry):
            for copy in loads(y):
                copy.wait()
            for w in range(2):
                o_buf[y, w] = w_buf[w, y].astype(bf16)
            store(y).start()
            return carry

        def finish(y, carry):
            store(y).wait()
            return carry

        lax.fori_loop(0, NY, begin, 0)
        lax.fori_loop(0, NY, one, 0)
        lax.fori_loop(0, NY, finish, 0)

    return pl.pallas_call(
        body,
        in_specs=[HBM] * 2,
        out_specs=HBM,
        out_shape=pltpu.HBM((NY, 2, FEAT, HID), bf16),
        scratch_shapes=[
            pltpu.VMEM((2, NY, FEAT, HID), f32),
            pltpu.VMEM((NY, 2, FEAT, HID), bf16),
            pltpu.SemaphoreType.DMA((2, NY)),
            pltpu.SemaphoreType.DMA((NY,)),
        ],
        compiler_params=MIDDLE,
    )(in_hbm(in_weight), in_hbm(out_weight_t))


def fill_order(place_ref, order_ref):
    def one(r, carry):
        at = pl.ds(pl.multiple_of(r * PAIR, PAIR), PAIR)
        place = jnp.concatenate([place_ref[at, :]] * (TOKENS // 128), axis=1)
        column = lax.broadcasted_iota(jnp.int32, (PAIR, TOKENS), 1)
        order_ref[at, :] = jnp.where(place == column, 1.0, 0.0).astype(bf16)
        return carry

    lax.fori_loop(0, TOKENS // PAIR, one, 0)


def behind(mine, step, size):
    return lax.rem(mine - step + size, size)


def sort_tokens(here, own, other, place):
    def body(here_ref, *refs):
        pieces, (p_ref, x_ref, t_ref, pair_ref) = refs[:8], refs[8:12]
        rows, place_buf, p_buf, x_buf, t_buf, pair_buf, in_sem, p_sem, x_sem, t_sem, pair_sem = refs[12:]

        def load(piece):
            o, u = divmod(piece, NX)
            core = here_ref[3] if o == 0 else 1 - here_ref[3]
            lane = pl.multiple_of((behind(here_ref[2], u, NX) * 2 + core) * 128, 128)
            return pltpu.make_async_copy(
                pieces[piece], rows.at[:, :, :, pl.ds(lane, 128)], in_sem.at[piece]
            )

        def stores(a, t):
            at = pl.ds(pl.multiple_of(t * TILE, TILE), TILE)
            return (
                pltpu.make_async_copy(x_buf.at[a, :, at], x_ref.at[a, :, at], x_sem.at[a, t]),
                pltpu.make_async_copy(t_buf.at[a, at], t_ref.at[a, at], t_sem.at[a, t]),
            )

        share = here_ref[2] * 2 + here_ref[3]
        pair_array = lax.div(share, 4)
        pair_row = lax.rem(share, 4) * PAIR_ROWS
        p_load = pltpu.make_async_copy(p_ref, place_buf, p_sem)
        pair_store = pltpu.make_async_copy(pair_buf, pair_ref, pair_sem)
        loads = [load(piece) for piece in range(8)]
        p_load.start()
        for copy in loads:
            copy.start()
        p_load.wait()
        fill_order(place_buf, p_buf)
        for copy in loads:
            copy.wait()

        def one(i, carry):
            a, t = lax.div(i, TILES), lax.rem(i, TILES)
            at = pl.ds(pl.multiple_of(t * TILE, TILE), TILE)
            given = rows[:, a].reshape(NY * FEAT, TOKENS)
            ordered = dot(given, p_buf[:, at], ((1,), (0,))).astype(bf16)
            x_buf[a, :, at] = ordered
            t_buf[a, at, :] = ordered.T

            @pl.when(a == pair_array)
            def _():
                for k in range(TILE // TOK_IMG):
                    start = t * TILE + k * TOK_IMG + pair_row
                    some = t_buf[a, pl.ds(pl.multiple_of(start, PAIR_ROWS), PAIR_ROWS), :]
                    image = ordered[:, k * TOK_IMG : (k + 1) * TOK_IMG]
                    pair_buf[TILE // TOK_IMG * t + k] = dot(some, image, ((1,), (0,)))

            for copy in stores(a, t):
                copy.start()
            return carry

        def finish(i, carry):
            for copy in stores(lax.div(i, TILES), lax.rem(i, TILES)):
                copy.wait()
            return carry

        lax.fori_loop(0, 2 * TILES, one, 0)
        pair_store.start()
        lax.fori_loop(0, 2 * TILES, finish, 0)
        pair_store.wait()

    feats, rows = (2, NY * FEAT, TOKENS), (2, TOKENS, NY * FEAT)
    pairs = (IMAGES, PAIR_ROWS, TOK_IMG)
    return pl.pallas_call(
        body,
        in_specs=[SMEM] + [HBM] * 9,
        out_specs=[HBM] * 3,
        out_shape=[pltpu.HBM(feats, bf16), pltpu.HBM(rows, bf16), pltpu.HBM(pairs, f32)],
        scratch_shapes=[
            pltpu.VMEM((NY, 2, FEAT, TOKENS), bf16),
            pltpu.VMEM((TOKENS, 128), jnp.int32),
            pltpu.VMEM((TOKENS, TOKENS), bf16),
            pltpu.VMEM(feats, bf16),
            pltpu.VMEM(rows, bf16),
            pltpu.VMEM(pairs, f32),
            pltpu.SemaphoreType.DMA((8,)),
            pltpu.SemaphoreType.DMA,
            pltpu.SemaphoreType.DMA((2, TILES)),
            pltpu.SemaphoreType.DMA((2, TILES)),
            pltpu.SemaphoreType.DMA,
        ],
        compiler_params=MIDDLE,
    )(here, *map(in_hbm, (*own, *other, place)))


def project(here, rows, weights):
    def body(here_ref, r_ref, w_ref, o_ref, r_buf, w_buf, o_buf, r_sem, w_sem, o_sem):
        w_loads = [
            pltpu.make_async_copy(
                w_ref.at[behind(here_ref[0], s, NY)], w_buf.at[:, s], w_sem.at[s]
            )
            for s in range(NY)
        ]

        def load(a):
            return pltpu.make_async_copy(r_ref.at[a], r_buf.at[a], r_sem.at[a])

        def store(a, t):
            part = (pl.ds(4 * t, 4), a)
            return pltpu.make_async_copy(o_buf.at[part], o_ref.at[part], o_sem.at[a, t])

        for copy in w_loads:
            copy.start()
        load(0).start()
        load(1).start()
        for copy in w_loads:
            copy.wait()
        load(0).wait()

        def one(i, carry):
            a, t = lax.div(i, TILES), lax.rem(i, TILES)

            @pl.when(i == TILES)
            def _():
                load(1).wait()

            at = pl.ds(pl.multiple_of(t * TILE, TILE), TILE)
            weight = w_buf[a].reshape(NY * FEAT, HID)
            scale = jnp.where(a == 0, f32(SCALE_IN), f32(SCALE_OUT))
            prod = dot(r_buf[a, at, :], weight, ((1,), (0,)))
            prod = (prod * scale).astype(bf16).reshape(4, TOK_IMG, HID)
            o_buf[pl.ds(4 * t, 4), a] = prod
            store(a, t).start()
            return carry

        def finish(i, carry):
            store(lax.div(i, TILES), lax.rem(i, TILES)).wait()
            return carry

        lax.fori_loop(0, 2 * TILES, one, 0, unroll=True)
        lax.fori_loop(0, 2 * TILES, finish, 0)

    given = (IMAGES, 2, TOK_IMG, HID)
    return pl.pallas_call(
        body,
        in_specs=[SMEM, HBM, ANY],
        out_specs=HBM,
        out_shape=pltpu.HBM(given, bf16),
        scratch_shapes=[
            pltpu.VMEM((2, TOKENS, NY * FEAT), bf16),
            pltpu.VMEM((2, NY, FEAT, HID), bf16),
            pltpu.VMEM(given, bf16),
            pltpu.SemaphoreType.DMA((2,)),
            pltpu.SemaphoreType.DMA((NY,)),
            pltpu.SemaphoreType.DMA((2, TILES)),
        ],
        compiler_params=MIDDLE,
    )(here, in_hbm(rows), weights)


def activate(here, summed, pairs):
    def body(here_ref, s_ref, p_ref, o_ref, n_ref):
        pre = s_ref[0:TOK_IMG, :].astype(f32)
        act, slope = gelu_and_slope(pre)
        act = act.astype(bf16)
        hid = (s_ref[TOK_IMG:, :].astype(f32) * slope).astype(bf16)
        o_ref[0:TOK_IMG, :] = act
        o_ref[TOK_IMG:, :] = hid
        both = dot(hid, hid, ((1,), (1,))) * p_ref[0:TOK_IMG] * (SCALE_IN * SCALE_IN)
        both += dot(act, act, ((1,), (1,))) * p_ref[TOK_IMG:] * (SCALE_OUT * SCALE_OUT)
        square = jnp.sum(jnp.sum(both, axis=0, keepdims=True), axis=1, keepdims=True)
        high = square.astype(bf16).astype(f32)
        middle = (square - high).astype(bf16).astype(f32)
        low = square - high - middle
        source = (here_ref[0] * NX + here_ref[2]) * 2 + here_ref[3]
        spot = lax.rem(source, 16) * IMAGES + here_ref[1]
        row = lax.broadcasted_iota(jnp.int32, (NORM_ROWS, 128), 0)
        lane = lax.broadcasted_iota(jnp.int32, (NORM_ROWS, 128), 1)
        kind = row - lax.div(source, 16) * 3
        value = jnp.where(kind == 0, high, jnp.where(kind == 1, middle, low))
        kept = (lane == spot) & (kind >= 0) & (kind < 3)
        n_ref[...] = jnp.where(kept, value, 0.0).astype(bf16)

    return pl.pallas_call(
        body,
        in_specs=[SMEM, VMEM, VMEM],
        out_specs=[VMEM, VMEM],
        out_shape=[
            jax.ShapeDtypeStruct((2 * TOK_IMG, HID), bf16),
            jax.ShapeDtypeStruct((NORM_ROWS, 128), bf16),
        ],
        compiler_params=SMALL,
    )(here, summed, pairs)


def all_grads(here, weights, feats, every, norms, place):
    rows = FEAT + NORM_ROWS

    def body(here_ref, w_ref, x_ref, e_ref, n_ref, p_ref, g_ref, own_ref, oth_ref, *refs):
        w_buf, x_buf, e_buf, n_buf, place_buf, p_buf, g_buf, o_buf = refs[:8]
        w_sem, x_sem, e_sem, n_sem, p_sem, g_sem, o_sem = refs[8:]
        w_load = pltpu.make_async_copy(w_ref.at[:, 0], w_buf, w_sem)
        n_load = pltpu.make_async_copy(n_ref, n_buf, n_sem)

        def e_load(w):
            part = pl.ds((1 - w) * TOK_IMG, TOK_IMG)
            return pltpu.make_async_copy(e_ref.at[:, part], e_buf.at[w], e_sem.at[w])

        def x_load(w):
            return pltpu.make_async_copy(x_ref.at[w], x_buf.at[w], x_sem.at[w])

        def g_stores(w):
            for s in range(NY):
                y = behind(here_ref[0], s, NY)
                yield pltpu.make_async_copy(g_buf.at[w, s], g_ref.at[y, w], g_sem.at[w, s])

        def stores(x):
            u = lax.rem(x - here_ref[2] + NX, NX)
            yield pltpu.make_async_copy(o_buf.at[1, u], oth_ref.at[u], o_sem.at[1, x])
            yield pltpu.make_async_copy(o_buf.at[0, u], own_ref.at[u], o_sem.at[0, x])

        p_load = pltpu.make_async_copy(p_ref, place_buf, p_sem)
        p_load.start()
        e_load(0).start()
        w_load.start()
        n_load.start()
        x_load(0).start()
        e_load(1).start()
        x_load(1).start()
        p_load.wait()
        fill_order(place_buf, p_buf)
        n_load.wait()
        norms = n_buf[0].astype(f32)
        for b in range(1, IMAGES):
            norms += n_buf[b].astype(f32)
        norms = norms.astype(bf16)
        e_load(0).wait()
        w_load.wait()

        def one(i, carry):
            at = pl.multiple_of(i * TILE, TILE)
            hidden = e_buf[0].reshape(TOKENS, HID)
            placed = dot(p_buf[pl.ds(at, TILE), :], hidden, ((1,), (0,))).astype(bf16)
            weight = w_buf[...].reshape(NY * FEAT, HID)
            grad = (dot(weight, placed, ((1,), (1,))) * SCALE_IN).astype(bf16)
            for k in range(TILE // PAIR):
                x = TILE // PAIR * i + k
                u = lax.rem(x - here_ref[2] + NX, NX)
                for core in range(2):
                    o = lax.rem(core + here_ref[3], 2)
                    lane = k * PAIR + core * 128
                    half = grad[:, lane : lane + 128]
                    for y in range(NY):
                        v = lax.rem(y - here_ref[0] + NY, NY)
                        o_buf[o, u, v, 0:FEAT, :] = half[y * FEAT : (y + 1) * FEAT]
                        o_buf[o, u, v, FEAT:, :] = norms
                for copy in stores(x):
                    copy.start()
            return carry

        lax.fori_loop(0, TILES, one, 0)
        tile = HID
        steps = HID // tile

        def two(i, carry):
            w, n = lax.div(i, steps), lax.rem(i, steps)

            @pl.when(n == 0)
            def _():
                x_load(w).wait()

            @pl.when(i == steps)
            def _():
                e_load(w).wait()

            cols = pl.ds(pl.multiple_of(n * tile, tile), tile)
            hidden = e_buf[w, :, :, cols].reshape(TOKENS, tile)
            scale = jnp.where(w == 0, f32(SCALE_IN), f32(SCALE_OUT))
            grad = dot(x_buf[w], hidden, ((1,), (0,))) * scale
            g_buf[w, :, :, cols] = grad.astype(bf16).reshape(NY, FEAT, tile)

            @pl.when(n == steps - 1)
            def _():
                for copy in g_stores(w):
                    copy.start()

            return carry

        lax.fori_loop(0, 2 * steps, two, 0)
        for x in range(NX):
            for copy in stores(x):
                copy.wait()
        for w in range(2):
            for copy in g_stores(w):
                copy.wait()

    sums = (NX, NY, rows, 128)
    grads = (NY, 2, FEAT, HID)
    return pl.pallas_call(
        body,
        in_specs=[SMEM] + [HBM] * 3 + [ANY, HBM],
        out_specs=[HBM] * 3,
        out_shape=[pltpu.HBM(shape, bf16) for shape in (grads, sums, sums)],
        scratch_shapes=[
            pltpu.VMEM((NY, FEAT, HID), bf16),
            pltpu.VMEM((2, NY * FEAT, TOKENS), bf16),
            pltpu.VMEM((2, IMAGES, TOK_IMG, HID), bf16),
            pltpu.VMEM((IMAGES, NORM_ROWS, 128), bf16),
            pltpu.VMEM((TOKENS, 128), jnp.int32),
            pltpu.VMEM((TOKENS, TOKENS), bf16),
            pltpu.VMEM((2, NY, FEAT, HID), bf16),
            pltpu.VMEM((2, *sums), bf16),
            pltpu.SemaphoreType.DMA,
            pltpu.SemaphoreType.DMA((2,)),
            pltpu.SemaphoreType.DMA((2,)),
            pltpu.SemaphoreType.DMA,
            pltpu.SemaphoreType.DMA,
            pltpu.SemaphoreType.DMA((2, NY)),
            pltpu.SemaphoreType.DMA((2, NX)),
        ],
        compiler_params=MIDDLE,
    )(here, in_hbm(weights), in_hbm(feats), in_hbm(every), norms, in_hbm(place))


def update(rate, in_weight, out_weight_t, grads):
    def body(rate_ref, a_ref, b_ref, g_ref, a_out, b_out, zero_out, *refs):
        w_buf, g_buf, w_sem, g_sem, o_sem = refs
        zero_out[...] = jnp.zeros((8, 128), f32)

        def loads(y):
            cols = pl.ds(pl.multiple_of(y * HID, HID), HID)
            return (
                pltpu.make_async_copy(g_ref.at[y], g_buf.at[y], g_sem.at[y]),
                pltpu.make_async_copy(a_ref.at[:, cols], w_buf.at[0, y], w_sem.at[0, y]),
                pltpu.make_async_copy(b_ref.at[:, cols], w_buf.at[1, y], w_sem.at[1, y]),
            )

        def stores(y):
            cols = pl.ds(pl.multiple_of(y * HID, HID), HID)
            return (
                pltpu.make_async_copy(w_buf.at[0, y], a_out.at[:, cols], o_sem.at[0, y]),
                pltpu.make_async_copy(w_buf.at[1, y], b_out.at[:, cols], o_sem.at[1, y]),
            )

        def begin(y, carry):
            for copy in loads(y):
                copy.start()
            return carry

        def one(y, carry):
            for copy in loads(y):
                copy.wait()
            for w in range(2):
                w_buf[w, y] = w_buf[w, y] - rate_ref[0] * g_buf[y, w].astype(f32)
            for copy in stores(y):
                copy.start()
            return carry

        def finish(y, carry):
            for copy in stores(y):
                copy.wait()
            return carry

        lax.fori_loop(0, NY, begin, 0)
        lax.fori_loop(0, NY, one, 0)
        lax.fori_loop(0, NY, finish, 0)

    return pl.pallas_call(
        body,
        in_specs=[SMEM, HBM, HBM, ANY],
        out_specs=[HBM, HBM, VMEM],
        out_shape=[pltpu.HBM(in_weight.shape, f32)] * 2
        + [jax.ShapeDtypeStruct((8, 128), f32)],
        scratch_shapes=[
            pltpu.VMEM((2, NY, FEAT, HID), f32),
            pltpu.VMEM((NY, 2, FEAT, HID), bf16),
            pltpu.SemaphoreType.DMA((2, NY)),
            pltpu.SemaphoreType.DMA((NY,)),
            pltpu.SemaphoreType.DMA((2, NY)),
        ],
        compiler_params=MIDDLE,
    )(rate, in_hbm(in_weight), in_hbm(out_weight_t), grads)


def gelu_and_slope(pre):
    phi = 0.5 * (1.0 + lax.erf(pre * root_half))
    return pre * phi, phi + pre * jnp.exp(-0.5 * pre * pre) * inv_root_tau


def exchange(value, axes):
    return lax.all_to_all(value, axes, 0, 0, tiled=True)


def swap_cores(value):
    return lax.ppermute(value, "core", [(0, 1), (1, 0)])


def ahead(value, axis, step):
    return lax.ppermute(value, axis, [(i, (i + step) % 4) for i in range(4)])


def ring_gather(value, axis):
    near, back, far = ahead(value, axis, 1), ahead(value, axis, 3), ahead(value, axis, 2)
    return [value, near, far, back]


def token_place(image_ids):
    at = jnp.arange(TOKENS)
    same = (image_ids[:, None] == image_ids[None, :]) & (at[None, :] < at[:, None])
    place = image_ids * TOK_IMG + jnp.sum(same.astype(jnp.int32), axis=1)
    return jnp.broadcast_to(place[:, None], (TOKENS, 128))


def ring_sum(chunks, axis):
    total = chunks[0].astype(f32)
    for s in (1, 3, 2):
        total += ahead(chunks[s], axis, s).astype(f32)
    return total


def shards(tokens, out_grad, image_ids, learn_rate, in_weight, out_weight):
    here = jnp.stack([lax.axis_index(a) for a in ("y", "z", "x", "core")]).astype(jnp.int32)
    out_weight_t = out_weight.T
    halves = split_hidden(in_weight, out_weight_t)
    along_y = jnp.stack(ring_gather(jnp.stack([tokens.T, out_grad.T]), "y"))
    halves, along_y = lax.optimization_barrier((halves, along_y))
    weights = exchange(halves.reshape(NY * 2 * FEAT, HID), "y").reshape(NY, 2, FEAT, HID)
    own = ring_gather(along_y, "x")
    place, own[1] = lax.optimization_barrier((token_place(image_ids), own[1]))
    other = [swap_cores(piece) for piece in own]
    feats, rows, pairs = sort_tokens(here, own, other, place)
    parts = project(here, rows, weights).reshape(IMAGES, 2 * TOK_IMG, HID)
    summed = lax.psum_scatter(parts, "z", scatter_dimension=0)
    pairs = exchange(pairs.reshape(IMAGES * PAIR_ROWS, TOK_IMG), "z")
    pairs = jnp.sum(pairs.reshape(NZ, PAIR_ROWS, TOK_IMG), axis=0)
    pairs = lax.all_gather(pairs, ("x", "core"), axis=0, tiled=True)
    sent, norms = activate(here, summed, pairs)
    every = lax.all_gather(sent, "z")
    norms = exchange(jnp.tile(norms, (NZ, 1)), "z").reshape(NZ, NORM_ROWS, 128)
    grads, mine, theirs = all_grads(here, weights, feats, every, norms, place)
    grads = exchange(grads.reshape(NY * 2 * FEAT, HID), "y").reshape(NY, 2, FEAT, HID)
    merged = (mine.astype(f32) + swap_cores(theirs).astype(f32)).astype(bf16)
    along_x = ring_sum(merged, "x").astype(bf16)
    in_next, out_next, zero = update(learn_rate, in_weight, out_weight_t, grads)
    got = ring_sum(along_x, "y") + zero[0, 0]
    input_grad = got[:FEAT].astype(bf16).T
    example_sq = jnp.sum(got[FEAT:].reshape(NORM_ROWS * 16, IMAGES), axis=0)
    example_norm = 0.5 * jnp.log(example_sq + 1e-06)
    return (input_grad, in_next, out_next.T, example_norm)


def solution(mesh):
    chips = Mesh(mesh.devices.reshape(NY, NZ, NX, 2), ("y", "z", "x", "core"))
    row, col = ("y", "z"), ("x", "core")
    placed = (P(col, row), P(col, row), P(), P(), P(row, col), P(col, row))
    return jax.shard_map(
        shards,
        mesh=chips,
        in_specs=placed,
        out_specs=(P(col, row), P(row, col), P(col, row), P()),
        check_vma=False,
    )
```

```python
import functools

import jax
import jax.numpy as jnp
from jax import lax
from jax.experimental import pallas as pl
from jax.experimental.pallas import tpu as pltpu
from jax.sharding import Mesh, PartitionSpec as P

D = 6144
FF = 24576
IMAGES = 8
TOK_IMG = 128
TOKENS = 1024
FEAT = 192
NY, NZ, NX = 4, 8, 4
HID = 768
SCALE_IN = D ** (-0.5)
SCALE_OUT = FF ** (-0.5)
NORM_ROWS = 16
PAIR_ROWS = 2 * TOK_IMG // 8

root_half = 0.7071067811865476
inv_root_tau = 0.3989422804014327

f32 = jnp.float32
bf16 = jnp.bfloat16
MIB = 1024 * 1024
SMALL = pltpu.CompilerParams(vmem_limit_bytes=8 * MIB)
MIDDLE = pltpu.CompilerParams(vmem_limit_bytes=24 * MIB)
WHOLE = pltpu.CompilerParams(vmem_limit_bytes=56 * MIB)
VMEM = pl.BlockSpec(memory_space=pltpu.VMEM)
SMEM = pl.BlockSpec(memory_space=pltpu.SMEM)
HBM = pl.BlockSpec(memory_space=pltpu.HBM)
ANY = pl.BlockSpec(memory_space=pl.ANY)
TILE = 4 * TOK_IMG
TILES = TOKENS // TILE
PAIR = 2 * TOK_IMG


def dot(left, right, dims):
    return lax.dot_general(left, right, (dims, ((), ())), preferred_element_type=f32)


def in_hbm(value):
    return pltpu.with_memory_space_constraint(value, pltpu.HBM)


def split_hidden(in_weight, out_weight_t):
    def body(a_ref, b_ref, o_ref, w_buf, o_buf, w_sem, o_sem):
        def loads(y):
            cols = pl.ds(pl.multiple_of(y * HID, HID), HID)
            return (
                pltpu.make_async_copy(a_ref.at[:, cols], w_buf.at[0, y], w_sem.at[0, y]),
                pltpu.make_async_copy(b_ref.at[:, cols], w_buf.at[1, y], w_sem.at[1, y]),
            )

        def store(y):
            return pltpu.make_async_copy(o_buf.at[y], o_ref.at[y], o_sem.at[y])

        def begin(y, carry):
            for copy in loads(y):
                copy.start()
            return carry

        def one(y, carry):
            for copy in loads(y):
                copy.wait()
            for w in range(2):
                o_buf[y, w] = w_buf[w, y].astype(bf16)
            store(y).start()
            return carry

        def finish(y, carry):
            store(y).wait()
            return carry

        lax.fori_loop(0, NY, begin, 0)
        lax.fori_loop(0, NY, one, 0)
        lax.fori_loop(0, NY, finish, 0)

    return pl.pallas_call(
        body,
        in_specs=[HBM] * 2,
        out_specs=HBM,
        out_shape=pltpu.HBM((NY, 2, FEAT, HID), bf16),
        scratch_shapes=[
            pltpu.VMEM((2, NY, FEAT, HID), f32),
            pltpu.VMEM((NY, 2, FEAT, HID), bf16),
            pltpu.SemaphoreType.DMA((2, NY)),
            pltpu.SemaphoreType.DMA((NY,)),
        ],
        compiler_params=MIDDLE,
    )(in_hbm(in_weight), in_hbm(out_weight_t))


def fill_order(place_ref, order_ref):
    def one(r, carry):
        at = pl.ds(pl.multiple_of(r * PAIR, PAIR), PAIR)
        place = jnp.concatenate([place_ref[at, :]] * (TOKENS // 128), axis=1)
        column = lax.broadcasted_iota(jnp.int32, (PAIR, TOKENS), 1)
        order_ref[at, :] = jnp.where(place == column, 1.0, 0.0).astype(bf16)
        return carry

    lax.fori_loop(0, TOKENS // PAIR, one, 0)


def behind(mine, step, size):
    return lax.rem(mine - step + size, size)


def sort_tokens(here, own, other, place):
    def body(here_ref, *refs):
        pieces, (p_ref, x_ref, t_ref, pair_ref) = refs[:8], refs[8:12]
        rows, place_buf, p_buf, x_buf, t_buf, pair_buf, in_sem, p_sem, x_sem, t_sem, pair_sem = refs[12:]

        def load(piece):
            o, u = divmod(piece, NX)
            core = here_ref[3] if o == 0 else 1 - here_ref[3]
            lane = pl.multiple_of((behind(here_ref[2], u, NX) * 2 + core) * 128, 128)
            return pltpu.make_async_copy(
                pieces[piece], rows.at[:, :, :, pl.ds(lane, 128)], in_sem.at[piece]
            )

        def stores(a, t):
            at = pl.ds(pl.multiple_of(t * TILE, TILE), TILE)
            return (
                pltpu.make_async_copy(x_buf.at[a, :, at], x_ref.at[a, :, at], x_sem.at[a, t]),
                pltpu.make_async_copy(t_buf.at[a, at], t_ref.at[a, at], t_sem.at[a, t]),
            )

        share = here_ref[2] * 2 + here_ref[3]
        pair_array = lax.div(share, 4)
        pair_row = lax.rem(share, 4) * PAIR_ROWS
        p_load = pltpu.make_async_copy(p_ref, place_buf, p_sem)
        pair_store = pltpu.make_async_copy(pair_buf, pair_ref, pair_sem)
        loads = [load(piece) for piece in range(8)]
        p_load.start()
        for copy in loads:
            copy.start()
        p_load.wait()
        fill_order(place_buf, p_buf)
        for copy in loads:
            copy.wait()

        def one(i, carry):
            a, t = lax.div(i, TILES), lax.rem(i, TILES)
            at = pl.ds(pl.multiple_of(t * TILE, TILE), TILE)
            given = rows[:, a].reshape(NY * FEAT, TOKENS)
            ordered = dot(given, p_buf[:, at], ((1,), (0,))).astype(bf16)
            x_buf[a, :, at] = ordered
            t_buf[a, at, :] = ordered.T

            @pl.when(a == pair_array)
            def _():
                for k in range(TILE // TOK_IMG):
                    start = t * TILE + k * TOK_IMG + pair_row
                    some = t_buf[a, pl.ds(pl.multiple_of(start, PAIR_ROWS), PAIR_ROWS), :]
                    image = ordered[:, k * TOK_IMG : (k + 1) * TOK_IMG]
                    pair_buf[TILE // TOK_IMG * t + k] = dot(some, image, ((1,), (0,)))

            for copy in stores(a, t):
                copy.start()
            return carry

        def finish(i, carry):
            for copy in stores(lax.div(i, TILES), lax.rem(i, TILES)):
                copy.wait()
            return carry

        lax.fori_loop(0, 2 * TILES, one, 0)
        pair_store.start()
        lax.fori_loop(0, 2 * TILES, finish, 0)
        pair_store.wait()

    feats, rows = (2, NY * FEAT, TOKENS), (2, TOKENS, NY * FEAT)
    pairs = (IMAGES, PAIR_ROWS, TOK_IMG)
    return pl.pallas_call(
        body,
        in_specs=[SMEM] + [HBM] * 9,
        out_specs=[HBM] * 3,
        out_shape=[pltpu.HBM(feats, bf16), pltpu.HBM(rows, bf16), pltpu.HBM(pairs, f32)],
        scratch_shapes=[
            pltpu.VMEM((NY, 2, FEAT, TOKENS), bf16),
            pltpu.VMEM((TOKENS, 128), jnp.int32),
            pltpu.VMEM((TOKENS, TOKENS), bf16),
            pltpu.VMEM(feats, bf16),
            pltpu.VMEM(rows, bf16),
            pltpu.VMEM(pairs, f32),
            pltpu.SemaphoreType.DMA((8,)),
            pltpu.SemaphoreType.DMA,
            pltpu.SemaphoreType.DMA((2, TILES)),
            pltpu.SemaphoreType.DMA((2, TILES)),
            pltpu.SemaphoreType.DMA,
        ],
        compiler_params=MIDDLE,
    )(here, *map(in_hbm, (*own, *other, place)))


def project(here, rows, weights):
    def body(here_ref, r_ref, w_ref, o_ref, r_buf, w_buf, o_buf, r_sem, w_sem, o_sem):
        w_loads = [
            pltpu.make_async_copy(
                w_ref.at[behind(here_ref[0], s, NY)], w_buf.at[:, s], w_sem.at[s]
            )
            for s in range(NY)
        ]

        def load(a):
            return pltpu.make_async_copy(r_ref.at[a], r_buf.at[a], r_sem.at[a])

        def store(a, t):
            part = (pl.ds(4 * t, 4), a)
            return pltpu.make_async_copy(o_buf.at[part], o_ref.at[part], o_sem.at[a, t])

        for copy in w_loads:
            copy.start()
        load(0).start()
        load(1).start()
        for copy in w_loads:
            copy.wait()
        load(0).wait()

        def one(i, carry):
            a, t = lax.div(i, TILES), lax.rem(i, TILES)

            @pl.when(i == TILES)
            def _():
                load(1).wait()

            at = pl.ds(pl.multiple_of(t * TILE, TILE), TILE)
            weight = w_buf[a].reshape(NY * FEAT, HID)
            scale = jnp.where(a == 0, f32(SCALE_IN), f32(SCALE_OUT))
            prod = dot(r_buf[a, at, :], weight, ((1,), (0,)))
            prod = (prod * scale).astype(bf16).reshape(4, TOK_IMG, HID)
            o_buf[pl.ds(4 * t, 4), a] = prod
            store(a, t).start()
            return carry

        def finish(i, carry):
            store(lax.div(i, TILES), lax.rem(i, TILES)).wait()
            return carry

        lax.fori_loop(0, 2 * TILES, one, 0, unroll=True)
        lax.fori_loop(0, 2 * TILES, finish, 0)

    given = (IMAGES, 2, TOK_IMG, HID)
    return pl.pallas_call(
        body,
        in_specs=[SMEM, HBM, ANY],
        out_specs=HBM,
        out_shape=pltpu.HBM(given, bf16),
        scratch_shapes=[
            pltpu.VMEM((2, TOKENS, NY * FEAT), bf16),
            pltpu.VMEM((2, NY, FEAT, HID), bf16),
            pltpu.VMEM(given, bf16),
            pltpu.SemaphoreType.DMA((2,)),
            pltpu.SemaphoreType.DMA((NY,)),
            pltpu.SemaphoreType.DMA((2, TILES)),
        ],
        compiler_params=MIDDLE,
    )(here, in_hbm(rows), weights)


def activate(here, summed, pairs):
    def body(here_ref, s_ref, p_ref, o_ref, n_ref, s_buf, o_buf, s_sem, o_sem):
        def load(a):
            part = pl.ds(a * TOK_IMG, TOK_IMG)
            return pltpu.make_async_copy(s_ref.at[part], s_buf.at[a], s_sem.at[a])

        def store(a):
            part = pl.ds(a * TOK_IMG, TOK_IMG)
            return pltpu.make_async_copy(o_buf.at[a], o_ref.at[part], o_sem.at[a])

        load(0).start()
        load(1).start()
        load(0).wait()
        act, slope = gelu_and_slope(s_buf[0].astype(f32))
        act = act.astype(bf16)
        o_buf[0] = act
        store(0).start()
        load(1).wait()
        hid = (s_buf[1].astype(f32) * slope).astype(bf16)
        o_buf[1] = hid
        store(1).start()
        both = dot(hid, hid, ((1,), (1,))) * p_ref[0:TOK_IMG] * (SCALE_IN * SCALE_IN)
        both += dot(act, act, ((1,), (1,))) * p_ref[TOK_IMG:] * (SCALE_OUT * SCALE_OUT)
        square = jnp.sum(jnp.sum(both, axis=0, keepdims=True), axis=1, keepdims=True)
        high = square.astype(bf16).astype(f32)
        middle = (square - high).astype(bf16).astype(f32)
        low = square - high - middle
        source = (here_ref[0] * NX + here_ref[2]) * 2 + here_ref[3]
        spot = lax.rem(source, 16) * IMAGES + here_ref[1]
        row = lax.broadcasted_iota(jnp.int32, (NORM_ROWS, 128), 0)
        lane = lax.broadcasted_iota(jnp.int32, (NORM_ROWS, 128), 1)
        kind = row - lax.div(source, 16) * 3
        value = jnp.where(kind == 0, high, jnp.where(kind == 1, middle, low))
        kept = (lane == spot) & (kind >= 0) & (kind < 3)
        n_ref[...] = jnp.where(kept, value, 0.0).astype(bf16)
        store(0).wait()
        store(1).wait()

    return pl.pallas_call(
        body,
        in_specs=[SMEM, HBM, VMEM],
        out_specs=[HBM, VMEM],
        out_shape=[
            pltpu.HBM((2 * TOK_IMG, HID), bf16),
            jax.ShapeDtypeStruct((NORM_ROWS, 128), bf16),
        ],
        scratch_shapes=[
            pltpu.VMEM((2, TOK_IMG, HID), bf16),
            pltpu.VMEM((2, TOK_IMG, HID), bf16),
            pltpu.SemaphoreType.DMA((2,)),
            pltpu.SemaphoreType.DMA((2,)),
        ],
        compiler_params=SMALL,
    )(here, in_hbm(summed), pairs)


def all_grads(here, weights, feats, every, norms, place):
    rows = FEAT + NORM_ROWS

    def body(here_ref, w_ref, x_ref, e_ref, n_ref, p_ref, g_ref, own_ref, oth_ref, *refs):
        w_buf, x_buf, e_buf, n_buf, place_buf, p_buf, g_buf, o_buf = refs[:8]
        w_sem, x_sem, e_sem, n_sem, p_sem, g_sem, o_sem = refs[8:]
        w_load = pltpu.make_async_copy(w_ref.at[:, 0], w_buf, w_sem)
        n_load = pltpu.make_async_copy(n_ref, n_buf, n_sem)

        def e_load(w):
            part = pl.ds((1 - w) * TOK_IMG, TOK_IMG)
            return pltpu.make_async_copy(e_ref.at[:, part], e_buf.at[w], e_sem.at[w])

        def x_load(w):
            return pltpu.make_async_copy(x_ref.at[w], x_buf.at[w], x_sem.at[w])

        def g_stores(w):
            for s in range(NY):
                y = behind(here_ref[0], s, NY)
                yield pltpu.make_async_copy(g_buf.at[w, s], g_ref.at[y, w], g_sem.at[w, s])

        def stores(x):
            u = lax.rem(x - here_ref[2] + NX, NX)
            yield pltpu.make_async_copy(o_buf.at[1, u], oth_ref.at[u], o_sem.at[1, x])
            yield pltpu.make_async_copy(o_buf.at[0, u], own_ref.at[u], o_sem.at[0, x])

        p_load = pltpu.make_async_copy(p_ref, place_buf, p_sem)
        p_load.start()
        e_load(0).start()
        w_load.start()
        n_load.start()
        x_load(0).start()
        e_load(1).start()
        x_load(1).start()
        p_load.wait()
        fill_order(place_buf, p_buf)
        n_load.wait()
        norms = n_buf[0].astype(f32)
        for b in range(1, IMAGES):
            norms += n_buf[b].astype(f32)
        norms = norms.astype(bf16)
        e_load(0).wait()
        w_load.wait()

        def one(i, carry):
            at = pl.multiple_of(i * TILE, TILE)
            hidden = e_buf[0].reshape(TOKENS, HID)
            placed = dot(p_buf[pl.ds(at, TILE), :], hidden, ((1,), (0,))).astype(bf16)
            weight = w_buf[...].reshape(NY * FEAT, HID)
            grad = (dot(weight, placed, ((1,), (1,))) * SCALE_IN).astype(bf16)
            for k in range(TILE // PAIR):
                x = TILE // PAIR * i + k
                u = lax.rem(x - here_ref[2] + NX, NX)
                for core in range(2):
                    o = lax.rem(core + here_ref[3], 2)
                    lane = k * PAIR + core * 128
                    half = grad[:, lane : lane + 128]
                    for y in range(NY):
                        v = lax.rem(y - here_ref[0] + NY, NY)
                        o_buf[o, u, v, 0:FEAT, :] = half[y * FEAT : (y + 1) * FEAT]
                        o_buf[o, u, v, FEAT:, :] = norms
                for copy in stores(x):
                    copy.start()
            return carry

        lax.fori_loop(0, TILES, one, 0)
        tile = HID
        steps = HID // tile

        def two(i, carry):
            w, n = lax.div(i, steps), lax.rem(i, steps)

            @pl.when(n == 0)
            def _():
                x_load(w).wait()

            @pl.when(i == steps)
            def _():
                e_load(w).wait()

            cols = pl.ds(pl.multiple_of(n * tile, tile), tile)
            hidden = e_buf[w, :, :, cols].reshape(TOKENS, tile)
            scale = jnp.where(w == 0, f32(SCALE_IN), f32(SCALE_OUT))
            grad = dot(x_buf[w], hidden, ((1,), (0,))) * scale
            g_buf[w, :, :, cols] = grad.astype(bf16).reshape(NY, FEAT, tile)

            @pl.when(n == steps - 1)
            def _():
                for copy in g_stores(w):
                    copy.start()

            return carry

        lax.fori_loop(0, 2 * steps, two, 0)
        for x in range(NX):
            for copy in stores(x):
                copy.wait()
        for w in range(2):
            for copy in g_stores(w):
                copy.wait()

    sums = (NX, NY, rows, 128)
    grads = (NY, 2, FEAT, HID)
    return pl.pallas_call(
        body,
        in_specs=[SMEM] + [HBM] * 3 + [ANY, HBM],
        out_specs=[HBM] * 3,
        out_shape=[pltpu.HBM(shape, bf16) for shape in (grads, sums, sums)],
        scratch_shapes=[
            pltpu.VMEM((NY, FEAT, HID), bf16),
            pltpu.VMEM((2, NY * FEAT, TOKENS), bf16),
            pltpu.VMEM((2, IMAGES, TOK_IMG, HID), bf16),
            pltpu.VMEM((IMAGES, NORM_ROWS, 128), bf16),
            pltpu.VMEM((TOKENS, 128), jnp.int32),
            pltpu.VMEM((TOKENS, TOKENS), bf16),
            pltpu.VMEM((2, NY, FEAT, HID), bf16),
            pltpu.VMEM((2, *sums), bf16),
            pltpu.SemaphoreType.DMA,
            pltpu.SemaphoreType.DMA((2,)),
            pltpu.SemaphoreType.DMA((2,)),
            pltpu.SemaphoreType.DMA,
            pltpu.SemaphoreType.DMA,
            pltpu.SemaphoreType.DMA((2, NY)),
            pltpu.SemaphoreType.DMA((2, NX)),
        ],
        compiler_params=MIDDLE,
    )(here, in_hbm(weights), in_hbm(feats), in_hbm(every), norms, in_hbm(place))


def update(rate, in_weight, out_weight_t, grads):
    def body(rate_ref, a_ref, b_ref, g_ref, a_out, b_out, zero_out, *refs):
        w_buf, g_buf, w_sem, g_sem, o_sem = refs
        zero_out[...] = jnp.zeros((8, 128), f32)

        def loads(y):
            cols = pl.ds(pl.multiple_of(y * HID, HID), HID)
            return (
                pltpu.make_async_copy(g_ref.at[y], g_buf.at[y], g_sem.at[y]),
                pltpu.make_async_copy(a_ref.at[:, cols], w_buf.at[0, y], w_sem.at[0, y]),
                pltpu.make_async_copy(b_ref.at[:, cols], w_buf.at[1, y], w_sem.at[1, y]),
            )

        def stores(y):
            cols = pl.ds(pl.multiple_of(y * HID, HID), HID)
            return (
                pltpu.make_async_copy(w_buf.at[0, y], a_out.at[:, cols], o_sem.at[0, y]),
                pltpu.make_async_copy(w_buf.at[1, y], b_out.at[:, cols], o_sem.at[1, y]),
            )

        def begin(y, carry):
            for copy in loads(y):
                copy.start()
            return carry

        def one(y, carry):
            for copy in loads(y):
                copy.wait()
            for w in range(2):
                w_buf[w, y] = w_buf[w, y] - rate_ref[0] * g_buf[y, w].astype(f32)
            for copy in stores(y):
                copy.start()
            return carry

        def finish(y, carry):
            for copy in stores(y):
                copy.wait()
            return carry

        lax.fori_loop(0, NY, begin, 0)
        lax.fori_loop(0, NY, one, 0)
        lax.fori_loop(0, NY, finish, 0)

    return pl.pallas_call(
        body,
        in_specs=[SMEM, HBM, HBM, ANY],
        out_specs=[HBM, HBM, VMEM],
        out_shape=[pltpu.HBM(in_weight.shape, f32)] * 2
        + [jax.ShapeDtypeStruct((8, 128), f32)],
        scratch_shapes=[
            pltpu.VMEM((2, NY, FEAT, HID), f32),
            pltpu.VMEM((NY, 2, FEAT, HID), bf16),
            pltpu.SemaphoreType.DMA((2, NY)),
            pltpu.SemaphoreType.DMA((NY,)),
            pltpu.SemaphoreType.DMA((2, NY)),
        ],
        compiler_params=MIDDLE,
    )(rate, in_hbm(in_weight), in_hbm(out_weight_t), grads)


def gelu_and_slope(pre):
    phi = 0.5 * (1.0 + lax.erf(pre * root_half))
    return pre * phi, phi + pre * jnp.exp(-0.5 * pre * pre) * inv_root_tau


def exchange(value, axes):
    return lax.all_to_all(value, axes, 0, 0, tiled=True)


def swap_cores(value):
    return lax.ppermute(value, "core", [(0, 1), (1, 0)])


def ahead(value, axis, step):
    return lax.ppermute(value, axis, [(i, (i + step) % 4) for i in range(4)])


def ring_gather(value, axis):
    near, back, far = ahead(value, axis, 1), ahead(value, axis, 3), ahead(value, axis, 2)
    return [value, near, far, back]


def token_place(image_ids):
    at = jnp.arange(TOKENS)
    same = (image_ids[:, None] == image_ids[None, :]) & (at[None, :] < at[:, None])
    place = image_ids * TOK_IMG + jnp.sum(same.astype(jnp.int32), axis=1)
    return jnp.broadcast_to(place[:, None], (TOKENS, 128))


def ring_sum(chunks, axis):
    total = chunks[0].astype(f32)
    for s in (1, 3, 2):
        total += ahead(chunks[s], axis, s).astype(f32)
    return total


def shards(tokens, out_grad, image_ids, learn_rate, in_weight, out_weight):
    here = jnp.stack([lax.axis_index(a) for a in ("y", "z", "x", "core")]).astype(jnp.int32)
    out_weight_t = out_weight.T
    halves = split_hidden(in_weight, out_weight_t)
    along_y = jnp.stack(ring_gather(jnp.stack([tokens.T, out_grad.T]), "y"))
    halves, along_y = lax.optimization_barrier((halves, along_y))
    weights = exchange(halves.reshape(NY * 2 * FEAT, HID), "y").reshape(NY, 2, FEAT, HID)
    own = ring_gather(along_y, "x")
    place, own[1] = lax.optimization_barrier((token_place(image_ids), own[1]))
    other = [swap_cores(piece) for piece in own]
    feats, rows, pairs = sort_tokens(here, own, other, place)
    parts = project(here, rows, weights).reshape(IMAGES, 2 * TOK_IMG, HID)
    summed = lax.psum_scatter(parts, "z", scatter_dimension=0)
    pairs = exchange(pairs.reshape(IMAGES * PAIR_ROWS, TOK_IMG), "z")
    pairs = jnp.sum(pairs.reshape(NZ, PAIR_ROWS, TOK_IMG), axis=0)
    pairs = lax.all_gather(pairs, ("x", "core"), axis=0, tiled=True)
    sent, norms = activate(here, summed, pairs)
    every = lax.all_gather(sent, "z")
    norms = exchange(jnp.tile(norms, (NZ, 1)), "z").reshape(NZ, NORM_ROWS, 128)
    grads, mine, theirs = all_grads(here, weights, feats, every, norms, place)
    grads = exchange(grads.reshape(NY * 2 * FEAT, HID), "y").reshape(NY, 2, FEAT, HID)
    merged = (mine.astype(f32) + swap_cores(theirs).astype(f32)).astype(bf16)
    along_x = ring_sum(merged, "x").astype(bf16)
    in_next, out_next, zero = update(learn_rate, in_weight, out_weight_t, grads)
    got = ring_sum(along_x, "y") + zero[0, 0]
    input_grad = got[:FEAT].astype(bf16).T
    example_sq = jnp.sum(got[FEAT:].reshape(NORM_ROWS * 16, IMAGES), axis=0)
    example_norm = 0.5 * jnp.log(example_sq + 1e-06)
    return (input_grad, in_next, out_next.T, example_norm)


def solution(mesh):
    chips = Mesh(mesh.devices.reshape(NY, NZ, NX, 2), ("y", "z", "x", "core"))
    row, col = ("y", "z"), ("x", "core")
    placed = (P(col, row), P(col, row), P(), P(), P(row, col), P(col, row))
    return jax.shard_map(
        shards,
        mesh=chips,
        in_specs=placed,
        out_specs=(P(col, row), P(row, col), P(col, row), P()),
        check_vma=False,
    )
```
